128 devices in a mesh: row: 8 (over z, core), col: 16 (over y, x).
Axes of the slice: x: 4, y: 4, z: 4, core: 2. Of those that a mesh axis runs over, the one named last changes fastest.
Arguments:
- current: float32 [4096, 128], P(('row', 'col')), may hold values from -6 to 6
- owner: int32 [4096], P(('row', 'col')), may hold values from 0 to 127, as said below
- voxel: int32 [4096, 128], P(('row', 'col')), may hold values from -1 to 65535, as said below
- material: int32 [4096, 128], P(('row', 'col')), may hold values from 0 to 7
- resist: float32 [8], replicated, may hold values from 0.5 to 4
- green: float32 [3, 2, 4096, 4096], P(None, None, ('row', 'col')), may hold values from -36 to 36
Outputs:
- image_rows: float32 [4096, 128], P(('row', 'col'))
The draws below stay inside these ranges and needn't reach their ends.
Inputs may be any that keep to these rules, and one draw needn't show every extreme that they name: The 32 blocks of one device name 32 different owners; one owner is named by a block of every device. `voxel`: A block's live rows come first, the rest hold -1; each block has between three quarters of 128 and 128 live rows, and every device has a block with 128 live rows. No two live rows of all blocks name the same cell of the same owner.
All inputs are finite; a program needn't handle non-finite values.
Results may differ from the reference program's by a relative error of at most 0.00005.
Values sent between devices are 32-bit elements; how exact they have to be, the bound alone decides.
A program may use at most 256 MiB of HBM per device.

```python
import math
import jax
import jax.numpy as jnp
from jax import lax

G = 2048
Z = 2
BR = 128
NB = 32
NMAT = 8
P_SIZE = 4096
NBT = 4096
N_ROW = 8
N_COL = 16


def owner_order(key_item):
    return jax.random.permutation(key_item, G // (N_ROW * N_COL) * Z * G)


def route_plan(key):
    devices = N_ROW * N_COL
    base = jax.random.fold_in(key, 7)
    split_keys = jax.random.split(base, 6)
    hot_owner = jax.random.randint(split_keys[0], (), 0, devices)
    weights = jax.random.randint(split_keys[1], (devices,), 1, 5)
    raw_scores = jax.random.randint(split_keys[2], (devices, devices), 0, 65536)
    owner_ids = jnp.arange(devices, dtype=jnp.int32)
    scores = raw_scores * weights[None, :] * 256 + owner_ids[None, :]
    scores = jnp.where(owner_ids[None, :] == hot_owner, 2 ** 30, scores)
    unused, chosen = lax.top_k(scores, NB)
    chosen = chosen.astype(jnp.int32)
    shuffle_keys = jax.random.randint(split_keys[3], (devices, NB), 0, 65536) * NB + jnp.arange(NB, dtype=jnp.int32)[None, :]
    placing = jnp.argsort(shuffle_keys, axis=1)
    chosen = jnp.take_along_axis(chosen, placing, axis=1)
    live_counts = jax.random.randint(split_keys[4], (devices, NB), BR - BR // 4, BR + 1)
    live_counts = jnp.where(chosen == hot_owner, BR, live_counts)
    orders = jax.vmap(owner_order)(jax.random.split(split_keys[5], devices)).astype(jnp.int32)
    senders = jnp.arange(devices, dtype=jnp.int32)[:, None, None]
    slot_ids = jnp.arange(BR, dtype=jnp.int32)[None, None, :]
    cells_taken = orders[chosen[:, :, None], senders * BR + slot_ids]
    voxels = jnp.where(slot_ids < live_counts[:, :, None], cells_taken, -1)
    return (chosen.reshape(devices * NB).astype(jnp.int32), voxels.reshape(devices * NB, BR).astype(jnp.int32))


def draw_owner(key, part):
    return route_plan(key)[0]


def draw_voxel(key, part):
    return route_plan(key)[1]


def plant(drawn, rng, low, high):
    dims = drawn.shape
    place = [jax.random.randint(jax.random.fold_in(rng, axis), (), 0, dims[axis]) for axis in range(len(dims))]
    drawn = drawn.at[tuple(place)].set(low)
    longest = dims.index(max(dims))
    place[longest] = (place[longest] + 1) % dims[longest]
    return drawn.at[tuple(place)].set(high)


def shard_levels(key, extent, pieces, low, high):
    factor_of, own = 1.0, jax.random.fold_in(key, 6)
    for dim, parts in pieces:
        heights = jnp.exp(jax.random.uniform(jax.random.fold_in(own, dim), (parts,), jnp.float32, low / len(pieces), high / len(pieces)))
        factor_of = factor_of * jnp.repeat(heights, extent[dim] // parts).reshape([-1 if axis == dim else 1 for axis in range(len(extent))])
    return factor_of


def gaussian(key, dims, deviation, reach, pieces=(), kind=jnp.bfloat16):
    entries = deviation * jax.random.normal(key, dims, jnp.float32)
    if pieces:
        entries = entries * shard_levels(key, dims, pieces, -0.22, 0.18)
    return jnp.clip(entries, -reach, reach).astype(kind)


def setup_inputs(seed: int = 0) -> dict:
    streams_of = jax.random.split(jax.random.key(seed), 7)
    return {
        "current": gaussian(streams_of[0], (NBT, BR), 1.0, 6.0, ((0, 128),), jnp.float32),
        "owner": draw_owner(jax.random.fold_in(streams_of[6], 71), 0),
        "voxel": draw_voxel(jax.random.fold_in(streams_of[6], 71), 0),
        "material": plant(jax.random.randint(streams_of[3], (NBT, BR), 0, NMAT), jax.random.fold_in(streams_of[3], 1), 0, NMAT - 1).astype(jnp.int32),
        "resist": jnp.clip(jnp.exp(jax.random.uniform(streams_of[4], (NMAT,), jnp.float32, math.log(0.5), math.log(4.0))), 0.5, 4.0),
        "green": gaussian(streams_of[5], (2 * Z - 1, 2, P_SIZE, P_SIZE), 6.0, 36.0, ((2, 128),), jnp.float32),
    }


def reference(current, owner, voxel, material, resist, green):
    length = 2 * G
    strip_rows = G // (N_ROW * N_COL)
    is_live = voxel >= 0
    in_slab = jnp.where(is_live, voxel, 0)
    column_x = owner[:, None] * strip_rows + in_slab // (Z * G)
    plane_z = (in_slab // G) % Z
    column_y = in_slab % G
    cell_count = Z * length * length
    cell_index = (plane_z * length + column_x) * length + column_y
    placed = jnp.where(is_live, cell_index, cell_count)
    loaded = jnp.where(is_live, current, jnp.zeros_like(current))
    source = jnp.zeros((cell_count,), jnp.float32).at[placed.reshape(-1)].add(loaded.reshape(-1), mode="drop")
    source = source.reshape(Z, length, length)
    spectrum = jnp.fft.fft2(source)
    kernel = (green[:, 0] + 1j * green[:, 1]).transpose(0, 2, 1)
    planes_out = []
    for target in range(Z):
        running = kernel[target + Z - 1] * spectrum[0]
        for anchor in range(1, Z):
            running = running + kernel[target - anchor + Z - 1] * spectrum[anchor]
        planes_out.append(running)
    mixed = jnp.stack(planes_out)
    volume = jnp.real(jnp.fft.ifft2(mixed)).astype(jnp.float32)
    coupled = volume.reshape(-1)[jnp.where(is_live, cell_index, 0)]
    rates = resist[material]
    return jnp.where(is_live, rates * current + coupled, jnp.zeros_like(current)).astype(jnp.float32)
```

```python
import functools
import math

import jax
import jax.numpy as jnp
import ml_dtypes
import numpy as np
from jax import lax
from jax.experimental import pallas as pl
from jax.experimental.pallas import tpu as pltpu
from jax.sharding import PartitionSpec as P

F32 = jnp.float32
BF16 = jnp.bfloat16
LANES = 128


def halves(table):
    high = table.astype(ml_dtypes.bfloat16)
    low = (table - high.astype(np.float64)).astype(ml_dtypes.bfloat16)
    return high, low


def stacked(table, axis):
    high, low = halves(table)
    return np.concatenate([high, high, low], axis=axis)


def angles(left, right, length):
    return 2.0 * math.pi * (np.outer(left, right) % length) / length


@functools.lru_cache(maxsize=None)
def tables():
    out = {}
    j32, a16, n128, n64, a32 = (np.arange(n) for n in (32, 16, 128, 64, 32))
    theta = angles(j32, a16, 32)
    out["y_first"] = stacked(np.concatenate([np.cos(theta), -np.sin(theta)], axis=0), 1)
    theta = angles(j32, n128, 4096)
    out["y_turn"] = np.stack([np.cos(theta), -np.sin(theta)]).astype(np.float32)
    theta = angles(n128, n128, 128)
    cosine, sine = np.cos(theta), np.sin(theta)
    out["y_second"] = stacked(np.block([[cosine, -sine], [sine, cosine]]), 0)
    out["y_back"] = stacked(np.concatenate([cosine, sine], axis=1), 1)
    theta = np.tile(angles(n128, j32, 4096), (1, 4))
    sign = np.where(np.arange(128) < 64, -1.0, 1.0)
    out["y_unturn"] = np.stack([np.cos(theta), np.sin(theta) * sign]).astype(np.float32)
    theta = angles(j32, a16, 32)
    last = np.zeros((4, 2, 2, 32, 4, 2, 16))
    for x in range(4):
        for z in range(2):
            last[x, 0, z, :, x, z, :] = np.cos(theta)
            last[x, 1, z, :, x, z, :] = -np.sin(theta)
    out["y_last"] = stacked(last.reshape(512, 128), 0)
    first = []
    final = []
    for b in range(64):
        theta = angles(n64, 64 * a32 + b, 4096)
        first.append(stacked(np.concatenate([np.cos(theta), np.sin(theta)], axis=1), 1))
        final.append(stacked(np.concatenate([np.cos(theta.T), np.sin(theta.T)], axis=1), 1))
    out["x_first"] = np.concatenate(first, axis=0)
    out["x_final"] = np.concatenate(final, axis=0)
    theta = angles(n64, n64, 64)
    out["x_mid"] = stacked(np.concatenate([np.cos(theta), np.sin(theta)], axis=1), 1)
    return out


def split(value):
    high = value.astype(BF16)
    return high, (value - high.astype(F32)).astype(BF16)


def lane_sign(shape, low, high):
    lane = lax.broadcasted_iota(jnp.int32, shape, 1)
    return jnp.where(lane % LANES < LANES // 2, low, high).astype(F32)


def paired(value, low):
    swapped = pltpu.roll(value, LANES // 2, 1) * lane_sign(value.shape, low, -low)
    high, rest = split(value)
    high_s, rest_s = split(swapped)
    return jnp.concatenate([high, high_s, rest, rest_s, high, high_s], axis=0)


def dot(left, right, dims=(((1,), (0,)), ((), ()))):
    return lax.dot_general(left, right, dims, preferred_element_type=F32)


def pack_kernel(owner_ref, current_ref, voxel_ref, values_ref, places_ref):
    blocks = current_ref.shape[0]
    voxel = voxel_ref[...]
    loaded = jnp.where(voxel >= 0, current_ref[...], 0.0)
    values = jnp.zeros(values_ref.shape, F32)
    places = jnp.full(places_ref.shape, -1, jnp.int32)
    ids = lax.broadcasted_iota(jnp.int32, values.shape, 0)
    for block in range(blocks):
        mine = ids == owner_ref[block]
        values = jnp.where(mine, loaded[block : block + 1], values)
        places = jnp.where(mine, voxel[block : block + 1], places)
    values_ref[...] = values
    places_ref[...] = places


def one_hot(index, count):
    ids = lax.broadcasted_iota(jnp.int32, (count, index.shape[1]), 0)
    return jnp.where(ids == index, 1.0, 0.0).astype(BF16)


def fill_kernel(values_ref, places_ref, first_ref, turn_ref, second_ref, send_ref, slab_ref, left_ref):
    slab_ref[...] = jnp.zeros_like(slab_ref)

    @pl.loop(0, 16)
    def _(step):
        rows = pl.ds(pl.multiple_of(step * 8, 8), 8)
        places = places_ref[rows, :]
        values = values_ref[rows, :]
        high = values.astype(BF16).astype(F32)
        low = values - high
        tops, spots = [], []
        ids = lax.broadcasted_iota(jnp.int32, (LANES, LANES), 0)
        for s in range(8):
            place = places[s : s + 1]
            tops.append(one_hot(place >> 7, 512))
            hit = ids == (place & 127)
            spots.append(
                jnp.concatenate(
                    [
                        jnp.where(hit, high[s : s + 1], 0.0).astype(BF16),
                        jnp.where(hit, low[s : s + 1], 0.0).astype(BF16),
                    ],
                    axis=0,
                )
            )
        top = jnp.concatenate(tops, axis=1)
        spot = jnp.concatenate(spots, axis=1)
        slab_ref[...] += dot(top, spot, (((1,), (1,)), ((), ())))

    slab = slab_ref[:, :LANES] + slab_ref[:, LANES:]
    wide = jnp.concatenate([slab[16 * i : 16 * i + 16] for i in range(32)], axis=1)
    high, low = split(wide)
    begun = dot(first_ref[...], jnp.concatenate([high, low, high], axis=0))
    turn_re, turn_im = turn_ref[0], turn_ref[1]
    for i in range(32):
        re = begun[:32, LANES * i : LANES * i + LANES]
        im = begun[32:, LANES * i : LANES * i + LANES]
        both = jnp.concatenate(
            [re * turn_re - im * turn_im, re * turn_im + im * turn_re], axis=1
        )
        high, low = split(both)
        left_ref[32 * i : 32 * i + 32, :] = jnp.concatenate([high, low, high], axis=1)
    spectra = dot(left_ref[...], second_ref[...])
    for x in range(16):
        part = spectra[64 * x : 64 * x + 64]
        part = jnp.concatenate([part[:, :LANES], part[:, LANES:]], axis=0)
        send_ref[pl.ds(x, LANES, stride=16), :] = part.T


def mix_kernel(pencil_ref, green_ref, first_ref, mid_ref, final_ref, send_ref, half_ref, back_ref, coef_ref):
    @pl.loop(0, 32)
    def _(tile):
        cols = pl.ds(pl.multiple_of(tile * LANES, LANES), LANES)
        rows = pl.ds(pl.multiple_of(tile * LANES, LANES), LANES)
        re = [green_ref[o, 0, :, cols] for o in range(3)]
        im = [green_ref[o, 1, :, cols] for o in range(3)]
        arranged = [
            [re[1], re[1], re[1], re[1]],
            [re[0], -im[2], re[0], im[2]],
            [-im[1], -im[1], im[1], im[1]],
            [-im[0], re[2], im[0], re[2]],
        ]
        for g in range(4):
            coef_ref[g, rows, :] = jnp.concatenate(arranged[g], axis=0).T

    for b in range(64):
        rows = pencil_ref[pl.ds(b, 32, stride=64), :]
        begun = dot(first_ref[64 * b : 64 * b + 64, :], paired(rows, 1.0))
        half_ref[pl.ds(b, 64, stride=64), :] = begun

    mid = mid_ref[...]
    for k in range(64):
        spectrum = dot(mid, paired(half_ref[64 * k : 64 * k + 64, :], 1.0))
        mixed = jnp.zeros_like(spectrum)
        for g in range(4):
            turned = spectrum if g == 0 else pltpu.roll(spectrum, LANES - 32 * g, 1)
            mixed = mixed + coef_ref[g, pl.ds(k, 64, stride=64), :] * turned
        back_ref[pl.ds(k, 64, stride=64), :] = dot(mid, paired(mixed, -1.0))

    for b in range(64):
        send_ref[pl.ds(b, 32, stride=64), :] = dot(
            final_ref[32 * b : 32 * b + 32, :], paired(back_ref[64 * b : 64 * b + 64, :], -1.0)
        )


def read_kernel(field_ref, places_ref, back_ref, unturn_ref, last_ref, picked_ref):
    back = back_ref[...]
    cosine, sine = unturn_ref[0], unturn_ref[1]
    pieces = []
    for quad in range(4):
        turned = []
        for i in range(4):
            rows = field_ref[pl.ds(4 * quad + i, LANES, stride=16), :]
            piece = dot(back, paired(rows, -1.0))
            turned.append(piece * cosine + pltpu.roll(piece, LANES // 2, 1) * sine)
        high, low = split(jnp.concatenate(turned, axis=1))
        pieces.append(dot(jnp.concatenate([high, low, high], axis=1), last_ref[...]))
    high, low = split(jnp.concatenate(pieces, axis=1) * (1.0 / 16777216.0))
    volume = jnp.concatenate([high, low], axis=0)
    ids = lax.broadcasted_iota(jnp.int32, (LANES, LANES), 0)

    @pl.loop(0, 16)
    def _(step):
        rows = pl.ds(pl.multiple_of(step * 8, 8), 8)
        places = places_ref[rows, :]
        top = jnp.concatenate([one_hot(places[s : s + 1] >> 7, 512) for s in range(8)], axis=1)
        found = dot(volume, top)
        lines = []
        for s in range(8):
            line = found[:LANES, LANES * s : LANES * s + LANES] + found[LANES:, LANES * s : LANES * s + LANES]
            line = jnp.where(ids == (places[s : s + 1] & 127), line, 0.0)
            lines.append(jnp.sum(line, axis=0, keepdims=True))
        picked_ref[rows, :] = jnp.concatenate(lines, axis=0)


def finish_kernel(owner_ref, resist_ref, returned_ref, current_ref, voxel_ref, material_ref, out_ref):
    blocks = current_ref.shape[0]
    material = material_ref[...]
    rates = jnp.zeros(current_ref.shape, F32)
    for kind in range(8):
        rates = jnp.where(material == kind, resist_ref[kind], rates)
    coupled = jnp.concatenate(
        [returned_ref[pl.ds(owner_ref[b], 1), :] for b in range(blocks)], axis=0
    )
    out_ref[...] = jnp.where(voxel_ref[...] >= 0, rates * current_ref[...] + coupled, 0.0)


VM = pl.BlockSpec(memory_space=pltpu.VMEM)
SM = pl.BlockSpec(memory_space=pltpu.SMEM)
PARAMS = pltpu.CompilerParams(vmem_limit_bytes=56 * 1024 * 1024)


def call(kernel, out, ins, scratch=()):
    return pl.pallas_call(
        kernel,
        out_shape=out,
        in_specs=ins,
        out_specs=jax.tree.map(lambda _: VM, out),
        scratch_shapes=list(scratch),
        compiler_params=PARAMS,
    )


def shards(current, owner, voxel, material, resist, green):
    shape = jax.ShapeDtypeStruct
    t = tables()
    axes = ("row", "col")
    swap = functools.partial(lax.all_to_all, axis_name=axes, split_axis=0, concat_axis=0, tiled=True)
    values, places = call(
        pack_kernel, (shape((128, 128), F32), shape((128, 128), jnp.int32)), [SM, VM, VM]
    )(owner, current, voxel)
    values, places = swap(values), swap(places)
    spread = call(
        fill_kernel,
        shape((2048, LANES), F32),
        [VM] * 5,
        [pltpu.VMEM((512, 256), F32), pltpu.VMEM((1024, 768), BF16)],
    )(values, places, t["y_first"], t["y_turn"], t["y_second"])
    pencil = swap(spread)
    field = call(
        mix_kernel,
        shape((2048, LANES), F32),
        [VM] * 5,
        [
            pltpu.VMEM((4096, LANES), F32),
            pltpu.VMEM((4096, LANES), F32),
            pltpu.VMEM((4, 4096, LANES), F32),
        ],
    )(pencil, green, t["x_first"], t["x_mid"], t["x_final"])
    field = swap(field)
    picked = call(read_kernel, shape((128, 128), F32), [VM] * 5)(
        field, places, t["y_back"], t["y_unturn"], t["y_last"]
    )
    returned = swap(picked)
    return call(finish_kernel, shape(current.shape, F32), [SM, SM, VM, VM, VM, VM])(
        owner, resist, returned, current, voxel, material
    )


def solution(mesh):
    in_specs = (
        P(("row", "col"), None),
        P(("row", "col")),
        P(("row", "col"), None),
        P(("row", "col"), None),
        P(),
        P(None, None, ("row", "col"), None),
    )
    out_specs = P(("row", "col"), None)
    return jax.shard_map(shards, mesh=mesh, in_specs=in_specs, out_specs=out_specs, check_vma=False)
```

```python
import functools
import math

import jax
import jax.numpy as jnp
import ml_dtypes
import numpy as np
from jax import lax
from jax.experimental import pallas as pl
from jax.experimental.pallas import tpu as pltpu
from jax.sharding import PartitionSpec as P

F32 = jnp.float32
BF16 = jnp.bfloat16
LANES = 128


def halves(table):
    high = table.astype(ml_dtypes.bfloat16)
    low = (table - high.astype(np.float64)).astype(ml_dtypes.bfloat16)
    return high, low


def stacked(table, axis):
    high, low = halves(table)
    return np.concatenate([high, high, low], axis=axis)


def angles(left, right, length):
    return 2.0 * math.pi * (np.outer(left, right) % length) / length


@functools.lru_cache(maxsize=None)
def tables():
    out = {}
    j32, a16, n128, n64, a32 = (np.arange(n) for n in (32, 16, 128, 64, 32))
    theta = angles(j32, a16, 32)
    out["y_first"] = stacked(np.concatenate([np.cos(theta), -np.sin(theta)], axis=0), 1)
    theta = angles(j32, n128, 4096)
    out["y_turn"] = np.stack([np.cos(theta), -np.sin(theta)]).astype(np.float32)
    theta = angles(n128, n128, 128)
    cosine, sine = np.cos(theta), np.sin(theta)
    out["y_second"] = stacked(np.block([[cosine, -sine], [sine, cosine]]), 0)
    out["y_back"] = stacked(np.concatenate([cosine, sine], axis=0), 1)
    theta = np.tile(angles(n128, j32, 4096), (1, 4))
    sign = np.where(np.arange(128) < 64, -1.0, 1.0)
    out["y_unturn"] = np.stack([np.cos(theta), np.sin(theta) * sign]).astype(np.float32)
    theta = angles(j32, a16, 32)
    last = np.zeros((4, 2, 2, 32, 4, 2, 16))
    for x in range(4):
        for z in range(2):
            last[x, 0, z, :, x, z, :] = np.cos(theta)
            last[x, 1, z, :, x, z, :] = -np.sin(theta)
    out["y_last"] = stacked(last.reshape(512, 128), 0)
    first = []
    final = []
    for b in range(64):
        theta = angles(n64, 64 * a32 + b, 4096)
        first.append(stacked(np.concatenate([np.cos(theta), np.sin(theta)], axis=0), 1))
        final.append(stacked(np.concatenate([np.cos(theta.T), np.sin(theta.T)], axis=0), 1))
    out["x_first"] = np.concatenate(first, axis=0)
    out["x_final"] = np.concatenate(final, axis=0)
    theta = angles(n64, n64, 64)
    out["x_mid"] = stacked(np.concatenate([np.cos(theta), np.sin(theta)], axis=0), 1)
    return out


def split(value):
    high = value.astype(BF16)
    return high, (value - high.astype(F32)).astype(BF16)


MESH = pl.DeviceIdType.MESH
ROWS, COLS, EDGE = 8, 16, 4
NAMES = (
    "y_first", "y_turn", "y_second", "x_first", "x_mid", "x_final", "y_back", "y_unturn", "y_last",
)


def dot(left, right, dims=(((1,), (0,)), ((), ()))):
    return lax.dot_general(left, right, dims, preferred_element_type=F32)


def triple(value):
    high, low = split(value)
    return jnp.concatenate([high, low, high], axis=0)


def combine(product, place, low):
    count = product.shape[0] // 2
    cosine = product[:count, LANES * place : LANES * place + LANES]
    sine = product[count:, LANES * place : LANES * place + LANES]
    lane = lax.broadcasted_iota(jnp.int32, (count, LANES), 1)
    sign = jnp.where(lane < LANES // 2, low, -low).astype(F32)
    return cosine + pltpu.roll(sine, LANES // 2, 1) * sign


def aligned(value, step):
    return pl.multiple_of(value * step, step)


def kernel(
    owner_ref, resist_ref, current_ref, voxel_ref, material_ref, green_hbm, *rest
):
    count = len(NAMES)
    tables_hbm, out_ref = rest[:count], rest[count]
    (
        green_ref, route_out, route_in, spread_ref, pencil_ref, field_out, field_in, picked_ref, returned_ref,
        slab_ref, top_ref, left_ref, half_ref, back_ref, coef_ref,
    ) = rest[count + 1 : count + 16]
    held = rest[count + 16 : 2 * count + 16]
    load_sems, send_sems, route_sems, pencil_sems, field_sem, return_sem, spread_gate = rest[2 * count + 16 :]
    first_y, turn_ref, second_y, first_x, mid_x, final_x, back_y, unturn_ref, last_y = held

    row, col = lax.axis_index("row"), lax.axis_index("col")
    me = row * COLS + col
    high_col, low_col = col // EDGE, col % EDGE

    barrier = pltpu.get_barrier_semaphore()
    for k in range(1, ROWS):
        pl.semaphore_signal(barrier, inc=1, device_id=((row + k) % ROWS, col), device_id_type=MESH)
    for k in range(1, COLS):
        pl.semaphore_signal(barrier, inc=1, device_id=(row, (col + k) % COLS), device_id_type=MESH)

    loads = [pltpu.make_async_copy(green_hbm, green_ref, load_sems.at[count])]
    loads += [pltpu.make_async_copy(tables_hbm[i], held[i], load_sems.at[i]) for i in range(count)]
    for load in loads:
        load.start()

    voxel = voxel_ref[...]
    live = voxel >= 0
    loaded = jnp.where(live, current_ref[...], 0.0)
    cells = voxel.astype(F32)
    values = jnp.zeros((ROWS * COLS, LANES), F32)
    places = jnp.full((ROWS * COLS, LANES), -1.0, F32)
    ids = lax.broadcasted_iota(jnp.int32, values.shape, 0)
    for block in range(current_ref.shape[0]):
        mine = ids == owner_ref[block]
        values = jnp.where(mine, loaded[block : block + 1], values)
        places = jnp.where(mine, cells[block : block + 1], places)
    route_out[pl.ds(0, ROWS * COLS, stride=2), :] = values
    route_out[pl.ds(1, ROWS * COLS, stride=2), :] = places
    slab_ref[...] = jnp.zeros_like(slab_ref)

    pl.semaphore_wait(barrier, ROWS + COLS - 2)
    for k in range(1, COLS):
        pl.semaphore_signal(spread_gate, inc=1, device_id=(row, (col + k) % COLS), device_id_type=MESH)
    pl.semaphore_wait(spread_gate, COLS - 1)

    def remote(source, target, size, device, send_sem, recv_sem):
        index = device[0] * COLS + device[1]
        return pltpu.make_async_remote_copy(
            source.at[pl.ds(index * size, size)],
            target.at[pl.ds(me * size, size)],
            send_sem,
            recv_sem,
            device_id=device,
            device_id_type=MESH,
        )

    def local(source, target, size, recv_sem):
        mine = pl.ds(me * size, size)
        return pltpu.make_async_copy(source.at[mine], target.at[mine], recv_sem)

    local(route_out, route_in, 2, route_sems.at[0]).start()

    @pl.loop(1, ROWS * COLS)
    def _(k):
        device = ((row + k // COLS) % ROWS, (col + k % COLS) % COLS)
        remote(route_out, route_in, 2, device, send_sems.at[0], route_sems.at[k // COLS]).start()

    side = lax.broadcasted_iota(jnp.int32, (256, LANES), 0).astype(F32).astype(BF16)
    one, zero = jnp.ones((256, LANES), BF16), jnp.zeros((256, LANES), BF16)

    def arrived(step):
        block = route_in[pl.ds(aligned((row - step + ROWS) % ROWS, 2 * COLS), 2 * COLS), :]
        place = block.astype(jnp.int32)
        top = jnp.where(place < 0, -1, (place >> 7) & 255).astype(F32).astype(BF16)
        spot = (((place >> 15) & 1) * LANES + (place & 127)).astype(F32).astype(BF16)
        return block, top, spot

    @pl.loop(0, ROWS)
    def _(step):
        pltpu.make_async_copy(
            route_in.at[pl.ds(0, 2 * COLS)], route_in.at[pl.ds(0, 2 * COLS)], route_sems.at[step]
        ).wait()
        block, top, spot = arrived(step)
        high, low = split(block)
        spots = []
        for s in range(COLS):
            top_ref[step, :, LANES * s : LANES * s + LANES] = jnp.where(
                side == top[2 * s + 1 : 2 * s + 2], one, zero
            )
            hit = side == spot[2 * s + 1 : 2 * s + 2]
            spots.append(
                jnp.concatenate(
                    [
                        jnp.where(hit, high[2 * s : 2 * s + 1], zero),
                        jnp.where(hit, low[2 * s : 2 * s + 1], zero),
                    ],
                    axis=0,
                )
            )
        slab_ref[...] += dot(jnp.concatenate(spots, axis=1), top_ref[step], (((1,), (1,)), ((), ())))

    for load in loads[1:]:
        load.wait()
    slab = (slab_ref[:256, :] + slab_ref[256:, :]).T
    wide = jnp.concatenate(
        [
            slab[16 * (i % 16) : 16 * (i % 16) + 16, LANES * (i // 16) : LANES * (i // 16) + LANES]
            for i in range(32)
        ],
        axis=1,
    )
    begun = dot(first_y[...], triple(wide))
    turn_re, turn_im = turn_ref[0], turn_ref[1]
    for i in range(32):
        re = begun[:32, LANES * i : LANES * i + LANES]
        im = begun[32:, LANES * i : LANES * i + LANES]
        both = jnp.concatenate([re * turn_re - im * turn_im, re * turn_im + im * turn_re], axis=1)
        high, low = split(both)
        left_ref[32 * i : 32 * i + 32, :] = jnp.concatenate([high, low, high], axis=1)
    spectra = dot(left_ref[...], second_y[...])
    for x in range(16):
        part = spectra[64 * x : 64 * x + 64]
        part = jnp.concatenate([part[:, :LANES], part[:, LANES:]], axis=0)
        spread_ref[pl.ds(x, LANES, stride=16), :] = part.T

    local(spread_ref, pencil_ref, 16, pencil_sems.at[low_col]).start()

    @pl.loop(1, ROWS * COLS)
    def _(k):
        turn = k // (ROWS * EDGE)
        device = (
            (row + (k // EDGE) % ROWS) % ROWS,
            ((high_col + k % EDGE) % EDGE) * EDGE + (low_col + turn) % EDGE,
        )
        remote(spread_ref, pencil_ref, 16, device, send_sems.at[1], pencil_sems.at[low_col]).start()

    loads[0].wait()

    @pl.loop(0, 32)
    def _(tile):
        cols = pl.ds(aligned(tile, LANES), LANES)
        re = [green_ref[o, 0, :, cols] for o in range(3)]
        im = [green_ref[o, 1, :, cols] for o in range(3)]
        arranged = [
            [re[1], re[1], re[1], re[1]],
            [re[0], -im[2], re[0], im[2]],
            [-im[1], -im[1], im[1], im[1]],
            [-im[0], re[2], im[0], re[2]],
        ]
        for g in range(4):
            turned = jnp.concatenate(arranged[g], axis=0).T
            coef_ref[g, pl.ds(2 * tile, 64, stride=64), :] = turned[:64]
            coef_ref[g, pl.ds(2 * tile + 1, 64, stride=64), :] = turned[64:]

    @pl.loop(0, EDGE)
    def _(turn):
        group = (low_col - turn + EDGE) % EDGE
        quarter = pl.ds(0, ROWS * EDGE * 16)
        pltpu.make_async_copy(pencil_ref.at[quarter], pencil_ref.at[quarter], pencil_sems.at[group]).wait()
        for i in range(16):
            b = group * 16 + i
            rows = pencil_ref[pl.ds(b, 32, stride=64), :]
            product = dot(first_x[pl.ds(aligned(b, 128), 128), :], triple(rows))
            half_ref[pl.ds(b, 64, stride=64), :] = combine(product, 0, 1.0)

    mid = mid_x[...]
    for start in range(0, 64, 8):
        ks = range(start, start + 8)
        product = dot(
            mid, jnp.concatenate([triple(half_ref[64 * k : 64 * k + 64, :]) for k in ks], axis=1)
        )
        mixed = []
        for i, k in enumerate(ks):
            spectrum = combine(product, i, 1.0)
            total = coef_ref[0, 64 * k : 64 * k + 64, :] * spectrum
            for g in range(1, 4):
                total = total + coef_ref[g, 64 * k : 64 * k + 64, :] * pltpu.roll(spectrum, LANES - 32 * g, 1)
            mixed.append(triple(total))
        product = dot(mid, jnp.concatenate(mixed, axis=1))
        for i, k in enumerate(ks):
            back_ref[pl.ds(k, 64, stride=64), :] = combine(product, i, -1.0)

    @pl.loop(0, EDGE)
    def _(turn):
        group = (low_col + turn) % EDGE
        for i in range(16):
            b = group * 16 + i
            rows = back_ref[pl.ds(aligned(b, 64), 64), :]
            product = dot(final_x[pl.ds(aligned(b, 64), 64), :], triple(rows))
            field_out[pl.ds(b, 32, stride=64), :] = combine(product, 0, -1.0)

        @pl.when(turn == 0)
        def _():
            local(field_out, field_in, 16, field_sem).start()

        @pl.loop(jnp.where(turn == 0, 1, 0), ROWS * EDGE)
        def _(k):
            device = ((row + k // EDGE) % ROWS, ((high_col + k % EDGE) % EDGE) * EDGE + group)
            remote(field_out, field_in, 16, device, send_sems.at[2], field_sem).start()

    pltpu.make_async_copy(field_in, field_in, field_sem).wait()

    back = back_y[...]
    cosine, sine = unturn_ref[0], unturn_ref[1]
    pieces = []
    for quad in range(4):
        product = dot(
            back,
            jnp.concatenate(
                [triple(field_in[pl.ds(4 * quad + i, LANES, stride=16), :]) for i in range(4)], axis=1
            ),
        )
        turned = []
        for i in range(4):
            piece = combine(product, i, -1.0)
            turned.append(piece * cosine + pltpu.roll(piece, LANES // 2, 1) * sine)
        high, low = split(jnp.concatenate(turned, axis=1))
        pieces.append(dot(jnp.concatenate([high, low, high], axis=1), last_y[...]))
    volume = jnp.concatenate(
        [jnp.concatenate(pieces[:2], axis=1), jnp.concatenate(pieces[2:], axis=1)], axis=0
    ) * (1.0 / 16777216.0)
    volume = jnp.concatenate(split(volume), axis=0)

    spots = lax.broadcasted_iota(jnp.int32, (256, LANES), 0)

    @pl.loop(0, ROWS)
    def _(step):
        base = (row - step + ROWS) % ROWS
        place = route_in[pl.ds(aligned(base, 2 * COLS), 2 * COLS), :].astype(jnp.int32)
        spot = ((place >> 15) & 1) * LANES + (place & 127)
        found = dot(volume, top_ref[step])
        lines = []
        for s in range(COLS):
            line = found[:256, LANES * s : LANES * s + LANES] + found[256:, LANES * s : LANES * s + LANES]
            line = jnp.where(spots == spot[2 * s + 1 : 2 * s + 2], line, 0.0)
            lines.append(jnp.sum(line, axis=0, keepdims=True))
        picked_ref[pl.ds(aligned(base, COLS), COLS), :] = jnp.concatenate(lines, axis=0)

        @pl.when(step == 0)
        def _():
            local(picked_ref, returned_ref, 1, return_sem).start()

        @pl.loop(jnp.where(step == 0, 1, 0), COLS)
        def _(k):
            device = (base, (col + k) % COLS)
            remote(picked_ref, returned_ref, 1, device, send_sems.at[3], return_sem).start()

    rates = jnp.zeros(current_ref.shape, F32)
    for kind in range(8):
        rates = jnp.where(material_ref[...] == kind, resist_ref[kind], rates)
    own = rates * current_ref[...]
    pltpu.make_async_copy(returned_ref, returned_ref, return_sem).wait()
    coupled = jnp.concatenate(
        [returned_ref[pl.ds(owner_ref[b], 1), :] for b in range(current_ref.shape[0])], axis=0
    )
    out_ref[...] = jnp.where(live, own + coupled, 0.0)
    for i, (ref, size) in enumerate(((route_out, 2), (spread_ref, 16), (field_out, 16), (picked_ref, 1))):
        sent = ref.at[pl.ds(0, (ROWS * COLS - 1) * size)]
        pltpu.make_async_copy(sent, sent, send_sems.at[i]).wait()


def shards(current, owner, voxel, material, resist, green):
    values = [jnp.asarray(tables()[name]) for name in NAMES]
    vmem, smem, anywhere = (
        pl.BlockSpec(memory_space=space) for space in (pltpu.VMEM, pltpu.SMEM, pl.ANY)
    )
    dma = pltpu.SemaphoreType.DMA
    shapes = [
        ((3, 2, 32, 4096), F32),
        ((256, LANES), F32),
        ((256, LANES), F32),
        ((2048, LANES), F32),
        ((2048, LANES), F32),
        ((2048, LANES), F32),
        ((2048, LANES), F32),
        ((128, LANES), F32),
        ((128, LANES), F32),
        ((512, 256), F32),
        ((ROWS, 256, 2048), BF16),
        ((1024, 768), BF16),
        ((4096, LANES), F32),
        ((4096, LANES), F32),
        ((4, 4096, LANES), F32),
    ] + [(value.shape, value.dtype) for value in values]
    return pl.pallas_call(
        kernel,
        out_shape=jax.ShapeDtypeStruct(current.shape, F32),
        in_specs=[smem, smem, vmem, vmem, vmem, anywhere] + [anywhere] * len(values),
        out_specs=vmem,
        scratch_shapes=[pltpu.VMEM(*shape) for shape in shapes]
        + [
            dma((len(values) + 1,)),
            dma((4,)),
            dma((ROWS,)),
            dma((EDGE,)),
            dma,
            dma,
            pltpu.SemaphoreType.REGULAR,
        ],
        compiler_params=pltpu.CompilerParams(
            collective_id=0, has_side_effects=True, vmem_limit_bytes=58 * 1024 * 1024
        ),
    )(owner, resist, current, voxel, material, green, *values)


def solution(mesh):
    in_specs = (
        P(("row", "col"), None),
        P(("row", "col")),
        P(("row", "col"), None),
        P(("row", "col"), None),
        P(),
        P(None, None, ("row", "col"), None),
    )
    out_specs = P(("row", "col"), None)
    return jax.shard_map(shards, mesh=mesh, in_specs=in_specs, out_specs=out_specs, check_vma=False)
```

```python
import functools
import math

import jax
import jax.numpy as jnp
import ml_dtypes
import numpy as np
from jax import lax
from jax.experimental import pallas as pl
from jax.experimental.pallas import tpu as pltpu
from jax.sharding import PartitionSpec as P

F32 = jnp.float32
BF16 = jnp.bfloat16
LANES = 128


def halves(table):
    high = table.astype(ml_dtypes.bfloat16)
    low = (table - high.astype(np.float64)).astype(ml_dtypes.bfloat16)
    return high, low


def stacked(table, axis):
    high, low = halves(table)
    return np.concatenate([high, high, low], axis=axis)


def angles(left, right, length):
    return 2.0 * math.pi * (np.outer(left, right) % length) / length


@functools.lru_cache(maxsize=None)
def tables():
    out = {}
    j32, a16, n128, n64, a32 = (np.arange(n) for n in (32, 16, 128, 64, 32))
    theta = angles(j32, a16, 32)
    out["y_first"] = stacked(np.concatenate([np.cos(theta), -np.sin(theta)], axis=0), 1)
    theta = angles(j32, n128, 4096)
    out["y_turn"] = np.stack([np.cos(theta), -np.sin(theta)]).astype(np.float32)
    theta = angles(n128, n128, 128)
    cosine, sine = np.cos(theta), np.sin(theta)
    out["y_second"] = stacked(np.block([[cosine, -sine], [sine, cosine]]), 0)
    out["y_back"] = stacked(np.concatenate([cosine, sine], axis=0), 1)
    theta = np.tile(angles(n128, j32, 4096), (1, 4))
    sign = np.where(np.arange(128) < 64, -1.0, 1.0)
    out["y_unturn"] = np.stack([np.cos(theta), np.sin(theta) * sign]).astype(np.float32)
    theta = angles(j32, a16, 32)
    last = np.zeros((4, 2, 2, 32, 4, 2, 16))
    for x in range(4):
        for z in range(2):
            last[x, 0, z, :, x, z, :] = np.cos(theta)
            last[x, 1, z, :, x, z, :] = -np.sin(theta)
    out["y_last"] = stacked(last.reshape(512, 128), 0)
    first = []
    final = []
    for b in range(64):
        theta = angles(n64, 64 * a32 + b, 4096)
        first.append(stacked(np.concatenate([np.cos(theta), np.sin(theta)], axis=0), 1))
        final.append(stacked(np.concatenate([np.cos(theta.T), np.sin(theta.T)], axis=0), 1))
    out["x_first"] = np.concatenate(first, axis=0)
    out["x_final"] = np.concatenate(final, axis=0)
    theta = angles(n64, n64, 64)
    out["x_mid"] = stacked(np.concatenate([np.cos(theta), np.sin(theta)], axis=0), 1)
    return out


def split(value):
    high = value.astype(BF16)
    return high, (value - high.astype(F32)).astype(BF16)


MESH = pl.DeviceIdType.MESH
ROWS, COLS, EDGE = 8, 16, 4
NAMES = (
    "y_first", "y_turn", "y_second", "x_first", "x_mid", "x_final", "y_back", "y_unturn", "y_last",
)


def dot(left, right, dims=(((1,), (0,)), ((), ()))):
    return lax.dot_general(left, right, dims, preferred_element_type=F32)


def triple(value):
    high, low = split(value)
    return jnp.concatenate([high, low, high], axis=0)


def combine(product, place, low):
    count = product.shape[0] // 2
    cosine = product[:count, LANES * place : LANES * place + LANES]
    sine = product[count:, LANES * place : LANES * place + LANES]
    lane = lax.broadcasted_iota(jnp.int32, (count, LANES), 1)
    sign = jnp.where(lane < LANES // 2, low, -low).astype(F32)
    return cosine + pltpu.roll(sine, LANES // 2, 1) * sign


def aligned(value, step):
    return pl.multiple_of(value * step, step)


def kernel(
    owner_ref, resist_ref, current_ref, voxel_ref, material_ref, green_hbm, *rest
):
    count = len(NAMES)
    tables_hbm, out_ref = rest[:count], rest[count]
    (
        green_ref, route_out, route_in, spread_ref, pencil_ref, field_out, field_in, picked_ref, returned_ref,
        slab_ref, top_ref, left_ref, half_ref, back_ref, coef_ref, volume_ref,
    ) = rest[count + 1 : count + 17]
    held = rest[count + 17 : 2 * count + 17]
    load_sems, send_sems, route_sems, pencil_sems, field_sems, return_sem, spread_gate = rest[2 * count + 17 :]
    first_y, turn_ref, second_y, first_x, mid_x, final_x, back_y, unturn_ref, last_y = held

    row, col = lax.axis_index("row"), lax.axis_index("col")
    me = row * COLS + col
    high_col, low_col = lax.div(col, EDGE), lax.rem(col, EDGE)

    barrier = pltpu.get_barrier_semaphore()
    for k in range(1, ROWS):
        pl.semaphore_signal(barrier, inc=1, device_id=(lax.rem(row + k, ROWS), col), device_id_type=MESH)
    for k in range(1, COLS):
        pl.semaphore_signal(barrier, inc=1, device_id=(row, lax.rem(col + k, COLS)), device_id_type=MESH)

    loads = [pltpu.make_async_copy(green_hbm, green_ref, load_sems.at[count])]
    loads += [pltpu.make_async_copy(tables_hbm[i], held[i], load_sems.at[i]) for i in range(count)]
    for load in loads:
        load.start()

    voxel = voxel_ref[...]
    live = voxel >= 0
    loaded = jnp.where(live, current_ref[...], 0.0)
    cells = voxel.astype(F32)
    values = jnp.zeros((ROWS * COLS, LANES), F32)
    places = jnp.full((ROWS * COLS, LANES), -1.0, F32)
    ids = lax.broadcasted_iota(jnp.int32, values.shape, 0)
    for block in range(current_ref.shape[0]):
        mine = ids == owner_ref[block]
        values = jnp.where(mine, loaded[block : block + 1], values)
        places = jnp.where(mine, cells[block : block + 1], places)
    route_out[pl.ds(0, ROWS * COLS, stride=2), :] = values
    route_out[pl.ds(1, ROWS * COLS, stride=2), :] = places
    pl.semaphore_wait(barrier, ROWS + COLS - 2)
    for k in range(1, COLS):
        pl.semaphore_signal(spread_gate, inc=1, device_id=(row, lax.rem(col + k, COLS)), device_id_type=MESH)
    def remote(source, target, size, device, send_sem, recv_sem, start=0, pitch=None):
        pitch = pitch or size
        index = device[0] * COLS + device[1]
        return pltpu.make_async_remote_copy(
            source.at[pl.ds(index * pitch + start, size)],
            target.at[pl.ds(me * pitch + start, size)],
            send_sem,
            recv_sem,
            device_id=device,
            device_id_type=MESH,
        )

    def local(source, target, size, recv_sem, start=0, pitch=None):
        mine = pl.ds(me * (pitch or size) + start, size)
        return pltpu.make_async_copy(source.at[mine], target.at[mine], recv_sem)

    def arrival(ref, rows, sem):
        part = ref.at[pl.ds(0, rows)]
        pltpu.make_async_copy(part, part, sem).wait()

    far = (2, 1, 3, 0)
    far_cols = [
        lax.rem(high_col + y, EDGE) * EDGE + lax.rem(low_col + x, EDGE) for y in far for x in far if (y, x) != (0, 0)
    ]
    next_cols = [lax.rem(col + k, COLS) for k in range(1, COLS)]

    def route(to_row, to_col, r):
        remote(route_out, route_in, 2, (to_row, to_col), send_sems.at[0], route_sems.at[r]).start()

    for to_col in next_cols:
        route(row, to_col, 0)
    local(route_out, route_in, 2, route_sems.at[0]).start()
    for r in range(1, ROWS):
        route(lax.rem(row + r, ROWS), col, r)
    pl.semaphore_wait(spread_gate, COLS - 1)

    @pl.loop(1, ROWS)
    def _(r):
        to_row = lax.rem(row + r, ROWS)
        for to_col in next_cols:
            route(to_row, to_col, r)

    def to_all(send):
        @pl.loop(0, ROWS)
        def _(k):
            core = lax.rem(row + 1 + lax.div(k, 4), 2)
            to_row = 2 * lax.rem(lax.div(row, 2) + 2 + 3 * lax.rem(k, 4), 4) + core
            for to_col in far_cols:
                send((to_row, to_col))

            @pl.when(to_row != row)
            def _():
                send((to_row, col))

    side = lax.broadcasted_iota(jnp.int32, (256, LANES), 0).astype(F32).astype(BF16)
    one, zero = jnp.ones((256, LANES), BF16), jnp.zeros((256, LANES), BF16)

    def asked(step):
        block = route_in[pl.ds(aligned(lax.rem(row - step + ROWS, ROWS), 2 * COLS), 2 * COLS), :]
        return block, block.astype(jnp.int32)

    for half in range(2):
        slab_ref[...] = jnp.zeros_like(slab_ref)

        @pl.loop(0, ROWS)
        def _(step):
            if half == 0:
                arrival(route_in, 2 * COLS, route_sems.at[step])
            block, place = asked(step)
            top = jnp.where(place < 0, -1, (place >> 7) & 255).astype(F32).astype(BF16)
            spot = jnp.where((place >> 15) == half, place & 127, -1).astype(F32).astype(BF16)
            high, low = split(block)
            spots = []
            for s in range(COLS):
                if half == 0:
                    top_ref[step, :, LANES * s : LANES * s + LANES] = jnp.where(
                        side == top[2 * s + 1 : 2 * s + 2], one, zero
                    )
                hit = side[:LANES] == spot[2 * s + 1 : 2 * s + 2]
                spots.append(
                    jnp.concatenate(
                        [
                            jnp.where(hit, high[2 * s : 2 * s + 1], zero[:LANES]),
                            jnp.where(hit, low[2 * s : 2 * s + 1], zero[:LANES]),
                        ],
                        axis=0,
                    )
                )
            slab_ref[...] += dot(jnp.concatenate(spots, axis=1), top_ref[step], (((1,), (1,)), ((), ())))

        if half == 0:
            for load in loads[1:]:
                load.wait()
        slab = (slab_ref[:LANES, :] + slab_ref[LANES:, :]).T
        wide = jnp.concatenate([slab[16 * i : 16 * i + 16] for i in range(16)], axis=1)
        begun = dot(first_y[...], triple(wide))
        turn_re, turn_im = turn_ref[0], turn_ref[1]
        for i in range(16):
            re = begun[:32, LANES * i : LANES * i + LANES]
            im = begun[32:, LANES * i : LANES * i + LANES]
            both = jnp.concatenate([re * turn_re - im * turn_im, re * turn_im + im * turn_re], axis=1)
            high, low = split(both)
            left_ref[32 * i : 32 * i + 32, :] = jnp.concatenate([high, low, high], axis=1)
        spectra = dot(left_ref[...], second_y[...])
        for x in range(8):
            part = spectra[64 * x : 64 * x + 64]
            part = jnp.concatenate([part[:, :LANES], part[:, LANES:]], axis=0)
            spread_ref[pl.ds(8 * half + x, LANES, stride=16), :] = part.T

        def send(device):
            remote(
                spread_ref, pencil_ref, 8, device, send_sems.at[1 + half], pencil_sems.at[half], 8 * half, 16
            ).start()

        to_all(send)
        local(spread_ref, pencil_ref, 8, pencil_sems.at[half], 8 * half, 16).start()

    loads[0].wait()

    @pl.loop(0, 32)
    def _(tile):
        cols = pl.ds(aligned(tile, LANES), LANES)
        re = [green_ref[o, 0, :, cols] for o in range(3)]
        im = [green_ref[o, 1, :, cols] for o in range(3)]
        arranged = [
            [re[1], re[1], re[1], re[1]],
            [re[0], -im[2], re[0], im[2]],
            [-im[1], -im[1], im[1], im[1]],
            [-im[0], re[2], im[0], re[2]],
        ]
        for g in range(4):
            turned = jnp.concatenate(arranged[g], axis=0).T
            coef_ref[g, pl.ds(2 * tile, 64, stride=64), :] = turned[:64]
            coef_ref[g, pl.ds(2 * tile + 1, 64, stride=64), :] = turned[64:]

    for half in range(2):
        arrival(pencil_ref, 1024, pencil_sems.at[half])
        for b in range(64):
            if (b % 16) // 8 == half:
                rows = pencil_ref[pl.ds(b, 32, stride=64), :]
                product = dot(first_x[128 * b : 128 * b + 128, :], triple(rows))
                half_ref[pl.ds(b, 64, stride=64), :] = combine(product, 0, 1.0)

    mid = mid_x[...]
    for start in range(0, 64, 8):
        ks = range(start, start + 8)
        product = dot(
            mid, jnp.concatenate([triple(half_ref[64 * k : 64 * k + 64, :]) for k in ks], axis=1)
        )
        mixed = []
        for i, k in enumerate(ks):
            spectrum = combine(product, i, 1.0)
            total = coef_ref[0, 64 * k : 64 * k + 64, :] * spectrum
            for g in range(1, 4):
                total = total + coef_ref[g, 64 * k : 64 * k + 64, :] * pltpu.roll(spectrum, LANES - 32 * g, 1)
            mixed.append(triple(total))
        product = dot(mid, jnp.concatenate(mixed, axis=1))
        for i, k in enumerate(ks):
            back_ref[pl.ds(k, 64, stride=64), :] = combine(product, i, -1.0)

    for half in range(2):
        for b in range(64):
            if (b % 16) // 8 == half:
                product = dot(final_x[64 * b : 64 * b + 64, :], triple(back_ref[64 * b : 64 * b + 64, :]))
                field_out[pl.ds(b, 32, stride=64), :] = combine(product, 0, -1.0)

        def send(device):
            remote(
                field_out, field_in, 8, device, send_sems.at[3 + half], field_sems.at[half], 8 * half, 16
            ).start()

        to_all(send)
        local(field_out, field_in, 8, field_sems.at[half], 8 * half, 16).start()

    cosine, sine = unturn_ref[0], unturn_ref[1]
    spots = lax.broadcasted_iota(jnp.int32, (LANES, LANES), 0)
    for half in range(2):
        arrival(field_in, 1024, field_sems.at[half])
        back = back_y[...]
        pieces = []
        for quad in range(2 * half, 2 * half + 2):
            product = dot(
                back,
                jnp.concatenate(
                    [triple(field_in[pl.ds(4 * quad + i, LANES, stride=16), :]) for i in range(4)], axis=1
                ),
            )
            turned = []
            for i in range(4):
                piece = combine(product, i, -1.0)
                turned.append(piece * cosine + pltpu.roll(piece, LANES // 2, 1) * sine)
            high, low = split(jnp.concatenate(turned, axis=1))
            pieces.append(dot(jnp.concatenate([high, low, high], axis=1), last_y[...]))
        volume_ref[...] = jnp.concatenate(split(jnp.concatenate(pieces, axis=1) * (1.0 / 16777216.0)), axis=0)

        @pl.loop(0, ROWS)
        def _(step):
            base = lax.rem(row - step + ROWS, ROWS)
            block, place = asked(step)
            spot = jnp.where((place >> 15) == half, place & 127, -1)
            found = dot(volume_ref[...], top_ref[step])
            lines = []
            for s in range(COLS):
                line = found[:LANES, LANES * s : LANES * s + LANES] + found[LANES:, LANES * s : LANES * s + LANES]
                line = jnp.where(spots == spot[2 * s + 1 : 2 * s + 2], line, 0.0)
                lines.append(jnp.sum(line, axis=0, keepdims=True))
            lines = jnp.concatenate(lines, axis=0)
            rows = pl.ds(aligned(base, COLS), COLS)
            if half == 0:
                picked_ref[rows, :] = lines
            else:
                picked_ref[rows, :] += lines

                @pl.when(step == 0)
                def _():
                    local(picked_ref, returned_ref, 1, return_sem).start()

                for to_col in next_cols:
                    remote(picked_ref, returned_ref, 1, (base, to_col), send_sems.at[5], return_sem).start()

                @pl.when(step > 0)
                def _():
                    remote(picked_ref, returned_ref, 1, (base, col), send_sems.at[5], return_sem).start()

    rates = jnp.zeros(current_ref.shape, F32)
    for kind in range(8):
        rates = jnp.where(material_ref[...] == kind, resist_ref[kind], rates)
    own = rates * current_ref[...]
    pltpu.make_async_copy(returned_ref, returned_ref, return_sem).wait()
    coupled = jnp.concatenate(
        [returned_ref[pl.ds(owner_ref[b], 1), :] for b in range(current_ref.shape[0])], axis=0
    )
    out_ref[...] = jnp.where(live, own + coupled, 0.0)
    for i, (ref, size) in enumerate(
        ((route_out, 2), (spread_ref, 8), (spread_ref, 8), (field_out, 8), (field_out, 8), (picked_ref, 1))
    ):
        arrival(ref, (ROWS * COLS - 1) * size, send_sems.at[i])


def shards(current, owner, voxel, material, resist, green):
    values = [jnp.asarray(tables()[name]) for name in NAMES]
    vmem, smem, anywhere = (
        pl.BlockSpec(memory_space=space) for space in (pltpu.VMEM, pltpu.SMEM, pl.ANY)
    )
    dma = pltpu.SemaphoreType.DMA
    shapes = [
        ((3, 2, 32, 4096), F32),
        ((256, LANES), F32),
        ((256, LANES), F32),
        ((2048, LANES), F32),
        ((2048, LANES), F32),
        ((2048, LANES), F32),
        ((2048, LANES), F32),
        ((128, LANES), F32),
        ((128, LANES), F32),
        ((256, 256), F32),
        ((ROWS, 256, 2048), BF16),
        ((512, 768), BF16),
        ((4096, LANES), F32),
        ((4096, LANES), F32),
        ((4, 4096, LANES), F32),
        ((256, 256), BF16),
    ] + [(value.shape, value.dtype) for value in values]
    return pl.pallas_call(
        kernel,
        out_shape=jax.ShapeDtypeStruct(current.shape, F32),
        in_specs=[smem, smem, vmem, vmem, vmem, anywhere] + [anywhere] * len(values),
        out_specs=vmem,
        scratch_shapes=[pltpu.VMEM(*shape) for shape in shapes]
        + [
            dma((len(values) + 1,)),
            dma((6,)),
            dma((ROWS,)),
            dma((2,)),
            dma((2,)),
            dma,
            pltpu.SemaphoreType.REGULAR,
        ],
        compiler_params=pltpu.CompilerParams(
            collective_id=0, has_side_effects=True, vmem_limit_bytes=58 * 1024 * 1024
        ),
    )(owner, resist, current, voxel, material, green, *values)


def solution(mesh):
    in_specs = (
        P(("row", "col"), None),
        P(("row", "col")),
        P(("row", "col"), None),
        P(("row", "col"), None),
        P(),
        P(None, None, ("row", "col"), None),
    )
    out_specs = P(("row", "col"), None)
    return jax.shard_map(shards, mesh=mesh, in_specs=in_specs, out_specs=out_specs, check_vma=False)
```

```python
import functools
import math

import jax
import jax.numpy as jnp
import ml_dtypes
import numpy as np
from jax import lax
from jax.experimental import pallas as pl
from jax.experimental.pallas import tpu as pltpu
from jax.sharding import PartitionSpec as P

F32 = jnp.float32
BF16 = jnp.bfloat16
LANES = 128


def halves(table):
    high = table.astype(ml_dtypes.bfloat16)
    low = (table - high.astype(np.float64)).astype(ml_dtypes.bfloat16)
    return high, low


def stacked(table, axis):
    high, low = halves(table)
    return np.concatenate([high, high, low], axis=axis)


def angles(left, right, length):
    return 2.0 * math.pi * (np.outer(left, right) % length) / length


@functools.lru_cache(maxsize=None)
def tables():
    out = {}
    j32, a16, n128, n64, a32 = (np.arange(n) for n in (32, 16, 128, 64, 32))
    theta = angles(j32, a16, 32)
    out["y_first"] = stacked(np.concatenate([np.cos(theta), -np.sin(theta)], axis=0), 1)
    theta = angles(j32, n128, 4096)
    out["y_turn"] = np.stack([np.cos(theta), -np.sin(theta)]).astype(np.float32)
    theta = angles(n128, n128, 128)
    cosine, sine = np.cos(theta), np.sin(theta)
    out["y_second"] = stacked(np.block([[cosine, -sine], [sine, cosine]]), 0)
    out["y_back"] = stacked(np.concatenate([cosine, sine], axis=0), 1)
    theta = np.tile(angles(n128, j32, 4096), (1, 4))
    sign = np.where(np.arange(128) < 64, -1.0, 1.0)
    out["y_unturn"] = np.stack([np.cos(theta), np.sin(theta) * sign]).astype(np.float32)
    theta = angles(j32, a16, 32)
    last = np.zeros((4, 2, 2, 32, 4, 2, 16))
    for x in range(4):
        for z in range(2):
            last[x, 0, z, :, x, z, :] = np.cos(theta)
            last[x, 1, z, :, x, z, :] = -np.sin(theta)
    out["y_last"] = stacked(last.reshape(512, 128), 0)
    first = []
    final = []
    for b in range(64):
        theta = angles(n64, 64 * a32 + b, 4096)
        first.append(stacked(np.concatenate([np.cos(theta), np.sin(theta)], axis=0), 1))
        final.append(stacked(np.concatenate([np.cos(theta.T), np.sin(theta.T)], axis=0), 1))
    out["x_first"] = np.concatenate(first, axis=0)
    out["x_final"] = np.concatenate(final, axis=0)
    theta = angles(n64, n64, 64)
    out["x_mid"] = stacked(np.concatenate([np.cos(theta), np.sin(theta)], axis=0), 1)
    return out


def split(value):
    high = value.astype(BF16)
    return high, (value - high.astype(F32)).astype(BF16)


MESH = pl.DeviceIdType.MESH
ROWS, COLS, EDGE = 8, 16, 4
PITCH, BLOCK = 72, 24
NAMES = (
    "y_first", "y_turn", "y_second", "x_first", "x_mid", "x_final", "y_back", "y_unturn", "y_last",
)


def dot(left, right, dims=(((1,), (0,)), ((), ()))):
    return lax.dot_general(left, right, dims, preferred_element_type=F32)


def triple(value):
    high, low = split(value)
    return jnp.concatenate([high, low, high], axis=0)


def combine(product, place, low):
    count = product.shape[0] // 2
    cosine = product[:count, LANES * place : LANES * place + LANES]
    sine = product[count:, LANES * place : LANES * place + LANES]
    lane = lax.broadcasted_iota(jnp.int32, (count, LANES), 1)
    sign = jnp.where(lane < LANES // 2, low, -low).astype(F32)
    return cosine + pltpu.roll(sine, LANES // 2, 1) * sign


def aligned(value, step):
    return pl.multiple_of(value * step, step)


def kernel(
    owner_ref, resist_ref, current_ref, voxel_ref, material_ref, green_hbm, *rest
):
    count = len(NAMES)
    tables_hbm, out_ref = rest[:count], rest[count]
    (
        green_ref, route_out, route_in, spread_ref, pencil_ref, field_out, field_in, picked_ref, returned_ref,
        slab_ref, top_ref, left_ref, half_ref, back_ref, coef_ref, volume_ref,
    ) = rest[count + 1 : count + 17]
    held = rest[count + 17 : 2 * count + 17]
    load_sems, send_sems, route_sems, pencil_sems, field_sems, return_sem, spread_gate = rest[2 * count + 17 :]
    first_y, turn_ref, second_y, first_x, mid_x, final_x, back_y, unturn_ref, last_y = held

    row, col = lax.axis_index("row"), lax.axis_index("col")
    me = row * COLS + col
    high_col, low_col = lax.div(col, EDGE), lax.rem(col, EDGE)

    barrier = pltpu.get_barrier_semaphore()
    for k in range(1, ROWS):
        pl.semaphore_signal(barrier, inc=1, device_id=(lax.rem(row + k, ROWS), col), device_id_type=MESH)
    for k in range(1, COLS):
        pl.semaphore_signal(barrier, inc=1, device_id=(row, lax.rem(col + k, COLS)), device_id_type=MESH)

    loads = [pltpu.make_async_copy(green_hbm, green_ref, load_sems.at[count])]
    loads += [pltpu.make_async_copy(tables_hbm[i], held[i], load_sems.at[i]) for i in range(count)]
    for load in loads:
        load.start()

    voxel = voxel_ref[...]
    live = voxel >= 0
    loaded = jnp.where(live, current_ref[...], 0.0)
    cells = voxel.astype(F32)
    values = jnp.zeros((ROWS * COLS, LANES), F32)
    places = jnp.full((ROWS * COLS, LANES), -1.0, F32)
    ids = lax.broadcasted_iota(jnp.int32, values.shape, 0)
    for block in range(current_ref.shape[0]):
        mine = ids == owner_ref[block]
        values = jnp.where(mine, loaded[block : block + 1], values)
        places = jnp.where(mine, cells[block : block + 1], places)
    route_out[pl.ds(0, ROWS * COLS, stride=2), :] = values
    route_out[pl.ds(1, ROWS * COLS, stride=2), :] = places
    pl.semaphore_wait(barrier, ROWS + COLS - 2)
    for k in range(1, COLS):
        pl.semaphore_signal(spread_gate, inc=1, device_id=(row, lax.rem(col + k, COLS)), device_id_type=MESH)
    def remote(source, start, target, place, size, device, send_sem, recv_sem):
        return pltpu.make_async_remote_copy(
            source.at[pl.ds(start, size)],
            target.at[pl.ds(place, size)],
            send_sem,
            recv_sem,
            device_id=device,
            device_id_type=MESH,
        )

    def local(source, start, target, place, size, recv_sem):
        return pltpu.make_async_copy(source.at[pl.ds(start, size)], target.at[pl.ds(place, size)], recv_sem)

    def outward(k, middle):
        return middle + (1 - 2 * lax.rem(k, 2)) * lax.div(k + 1, 2)

    def in_row(to_col):
        return lax.div(to_col, EDGE) * PITCH + lax.rem(to_col, EDGE) * 16

    own_x = row * (EDGE * PITCH) + in_row(col)
    own_block = me * BLOCK

    def arrival(ref, rows, sem):
        part = ref.at[pl.ds(0, rows)]
        pltpu.make_async_copy(part, part, sem).wait()

    far = (2, 1, 3, 0)
    far_cols = [
        lax.rem(high_col + y, EDGE) * EDGE + lax.rem(low_col + x, EDGE) for y in far for x in far if (y, x) != (0, 0)
    ]
    far_places = [in_row(to_col) for to_col in far_cols]
    own_place = in_row(col)
    next_cols = [lax.rem(col + k, COLS) for k in range(1, COLS)]

    def route(to_row, to_col, r):
        start = 2 * (to_row * COLS + to_col)
        remote(route_out, start, route_in, 2 * me, 2, (to_row, to_col), send_sems.at[0], route_sems.at[r]).start()

    for to_col in next_cols:
        route(row, to_col, 0)
    local(route_out, 2 * me, route_in, 2 * me, 2, route_sems.at[0]).start()
    for r in range(1, ROWS):
        route(lax.rem(row + r, ROWS), col, r)
    pl.semaphore_wait(spread_gate, COLS - 1)

    @pl.loop(0, ROWS - 1)
    def _(k):
        r = outward(k, ROWS // 2)
        to_row = lax.rem(row + r, ROWS)
        for to_col in far_cols:
            route(to_row, to_col, r)

    def to_all(send):
        @pl.loop(0, ROWS)
        def _(k):
            core = lax.rem(row + 1 + lax.div(k, 4), 2)
            to_row = 2 * lax.rem(lax.div(row, 2) + outward(lax.rem(k, 4), 2), 4) + core
            for to_col, place in zip(far_cols, far_places):
                send(to_row, to_col, place)

            @pl.when(to_row != row)
            def _():
                send(to_row, col, own_place)

    side = lax.broadcasted_iota(jnp.int32, (256, LANES), 0).astype(F32).astype(BF16)
    one, zero = jnp.ones((256, LANES), BF16), jnp.zeros((256, LANES), BF16)

    def asked(step):
        block = route_in[pl.ds(aligned(lax.rem(row - step + ROWS, ROWS), 2 * COLS), 2 * COLS), :]
        return block, block.astype(jnp.int32)

    for half in range(2):
        slab_ref[...] = jnp.zeros_like(slab_ref)

        @pl.loop(0, ROWS)
        def _(k):
            step = lax.rem(outward(lax.rem(k + ROWS - 1, ROWS), ROWS // 2), ROWS)
            if half == 0:
                arrival(route_in, 2 * COLS, route_sems.at[step])
            block, place = asked(step)
            top = jnp.where(place < 0, -1, (place >> 7) & 255).astype(F32).astype(BF16)
            spot = jnp.where((place >> 15) == half, place & 127, -1).astype(F32).astype(BF16)
            high, low = split(block)
            spots = []
            for s in range(COLS):
                if half == 0:
                    top_ref[step, :, LANES * s : LANES * s + LANES] = jnp.where(
                        side == top[2 * s + 1 : 2 * s + 2], one, zero
                    )
                hit = side[:LANES] == spot[2 * s + 1 : 2 * s + 2]
                spots.append(
                    jnp.concatenate(
                        [
                            jnp.where(hit, high[2 * s : 2 * s + 1], zero[:LANES]),
                            jnp.where(hit, low[2 * s : 2 * s + 1], zero[:LANES]),
                        ],
                        axis=0,
                    )
                )
            slab_ref[...] += dot(jnp.concatenate(spots, axis=1), top_ref[step], (((1,), (1,)), ((), ())))

        if half == 0:
            for load in loads[1:]:
                load.wait()
        slab = (slab_ref[:LANES, :] + slab_ref[LANES:, :]).T
        wide = jnp.concatenate([slab[16 * i : 16 * i + 16] for i in range(16)], axis=1)
        begun = dot(first_y[...], triple(wide))
        turn_re, turn_im = turn_ref[0], turn_ref[1]
        for i in range(16):
            re = begun[:32, LANES * i : LANES * i + LANES]
            im = begun[32:, LANES * i : LANES * i + LANES]
            both = jnp.concatenate([re * turn_re - im * turn_im, re * turn_im + im * turn_re], axis=1)
            high, low = split(both)
            left_ref[32 * i : 32 * i + 32, :] = jnp.concatenate([high, low, high], axis=1)
        spectra = dot(left_ref[...], second_y[...])
        for x in range(8):
            part = spectra[64 * x : 64 * x + 64]
            part = jnp.concatenate([part[:, :LANES], part[:, LANES:]], axis=0)
            spread_ref[pl.ds(8 * half + x, LANES, stride=BLOCK), :] = part.T

        def send(to_row, to_col, place):
            start = pl.multiple_of((to_row * COLS + to_col) * BLOCK + 8 * half, 8)
            remote(
                spread_ref, start, pencil_ref, pl.multiple_of(own_x + 8 * half, 8), 8, (to_row, to_col),
                send_sems.at[1 + half], pencil_sems.at[half],
            ).start()

        to_all(send)
        local(
            spread_ref, pl.multiple_of(own_block + 8 * half, 8), pencil_ref, pl.multiple_of(own_x + 8 * half, 8), 8,
            pencil_sems.at[half],
        ).start()

    loads[0].wait()

    @pl.loop(0, 32)
    def _(tile):
        cols = pl.ds(aligned(tile, LANES), LANES)
        re = [green_ref[o, 0, :, cols] for o in range(3)]
        im = [green_ref[o, 1, :, cols] for o in range(3)]
        arranged = [
            [re[1], re[1], re[1], re[1]],
            [re[0], -im[2], re[0], im[2]],
            [-im[1], -im[1], im[1], im[1]],
            [-im[0], re[2], im[0], re[2]],
        ]
        for g in range(4):
            turned = jnp.concatenate(arranged[g], axis=0).T
            coef_ref[g, pl.ds(2 * tile, 64, stride=PITCH), :] = turned[:64]
            coef_ref[g, pl.ds(2 * tile + 1, 64, stride=PITCH), :] = turned[64:]

    for half in range(2):
        arrival(pencil_ref, 1024, pencil_sems.at[half])
        for b in range(64):
            if (b % 16) // 8 == half:
                rows = pencil_ref[pl.ds(b, 32, stride=PITCH), :]
                product = dot(first_x[128 * b : 128 * b + 128, :], triple(rows))
                half_ref[pl.ds(b, 64, stride=PITCH), :] = combine(product, 0, 1.0)

    mid = mid_x[...]
    for start in range(0, 64, 8):
        ks = range(start, start + 8)
        product = dot(
            mid, jnp.concatenate([triple(half_ref[PITCH * k : PITCH * k + 64, :]) for k in ks], axis=1)
        )
        mixed = []
        for i, k in enumerate(ks):
            spectrum = combine(product, i, 1.0)
            total = coef_ref[0, PITCH * k : PITCH * k + 64, :] * spectrum
            for g in range(1, 4):
                total = total + coef_ref[g, PITCH * k : PITCH * k + 64, :] * pltpu.roll(spectrum, LANES - 32 * g, 1)
            mixed.append(triple(total))
        product = dot(mid, jnp.concatenate(mixed, axis=1))
        for i, k in enumerate(ks):
            back_ref[pl.ds(k, 64, stride=PITCH), :] = combine(product, i, -1.0)

    for half in range(2):
        for b in range(64):
            if (b % 16) // 8 == half:
                product = dot(final_x[64 * b : 64 * b + 64, :], triple(back_ref[PITCH * b : PITCH * b + 64, :]))
                field_out[pl.ds(b, 32, stride=PITCH), :] = combine(product, 0, -1.0)

        def send(to_row, to_col, place):
            start = pl.multiple_of(to_row * (EDGE * PITCH) + place + 8 * half, 8)
            remote(
                field_out, start, field_in, pl.multiple_of(own_block + 8 * half, 8), 8, (to_row, to_col),
                send_sems.at[3 + half], field_sems.at[half],
            ).start()

        to_all(send)
        local(
            field_out, pl.multiple_of(own_x + 8 * half, 8), field_in, pl.multiple_of(own_block + 8 * half, 8), 8,
            field_sems.at[half],
        ).start()

    cosine, sine = unturn_ref[0], unturn_ref[1]
    spots = lax.broadcasted_iota(jnp.int32, (LANES, LANES), 0)
    for half in range(2):
        arrival(field_in, 1024, field_sems.at[half])
        back = back_y[...]
        pieces = []
        for quad in range(2 * half, 2 * half + 2):
            product = dot(
                back,
                jnp.concatenate(
                    [triple(field_in[pl.ds(4 * quad + i, LANES, stride=BLOCK), :]) for i in range(4)], axis=1
                ),
            )
            turned = []
            for i in range(4):
                piece = combine(product, i, -1.0)
                turned.append(piece * cosine + pltpu.roll(piece, LANES // 2, 1) * sine)
            high, low = split(jnp.concatenate(turned, axis=1))
            pieces.append(dot(jnp.concatenate([high, low, high], axis=1), last_y[...]))
        volume_ref[...] = jnp.concatenate(split(jnp.concatenate(pieces, axis=1) * (1.0 / 16777216.0)), axis=0)

        @pl.loop(0, ROWS)
        def _(k):
            step = outward(k, ROWS // 2)
            base = lax.rem(row - step + ROWS, ROWS)
            block, place = asked(step)
            spot = jnp.where((place >> 15) == half, place & 127, -1)
            found = dot(volume_ref[...], top_ref[step])
            lines = []
            for s in range(COLS):
                line = found[:LANES, LANES * s : LANES * s + LANES] + found[LANES:, LANES * s : LANES * s + LANES]
                line = jnp.where(spots == spot[2 * s + 1 : 2 * s + 2], line, 0.0)
                lines.append(jnp.sum(line, axis=0, keepdims=True))
            lines = jnp.concatenate(lines, axis=0)
            rows = pl.ds(aligned(base, COLS), COLS)
            if half == 0:
                picked_ref[rows, :] = lines
            else:
                picked_ref[rows, :] += lines

                @pl.when(k == ROWS - 1)
                def _():
                    local(picked_ref, me, returned_ref, me, 1, return_sem).start()

                for to_col in far_cols:
                    remote(
                        picked_ref, base * COLS + to_col, returned_ref, me, 1, (base, to_col), send_sems.at[5], return_sem
                    ).start()

                @pl.when(k < ROWS - 1)
                def _():
                    remote(
                        picked_ref, base * COLS + col, returned_ref, me, 1, (base, col), send_sems.at[5], return_sem
                    ).start()

    rates = jnp.zeros(current_ref.shape, F32)
    for kind in range(8):
        rates = jnp.where(material_ref[...] == kind, resist_ref[kind], rates)
    own = rates * current_ref[...]
    pltpu.make_async_copy(returned_ref, returned_ref, return_sem).wait()
    coupled = jnp.concatenate(
        [returned_ref[pl.ds(owner_ref[b], 1), :] for b in range(current_ref.shape[0])], axis=0
    )
    out_ref[...] = jnp.where(live, own + coupled, 0.0)
    for i, (ref, size) in enumerate(
        ((route_out, 2), (spread_ref, 8), (spread_ref, 8), (field_out, 8), (field_out, 8), (picked_ref, 1))
    ):
        arrival(ref, (ROWS * COLS - 1) * size, send_sems.at[i])


def shards(current, owner, voxel, material, resist, green):
    values = [jnp.asarray(tables()[name]) for name in NAMES]
    vmem, smem, anywhere = (
        pl.BlockSpec(memory_space=space) for space in (pltpu.VMEM, pltpu.SMEM, pl.ANY)
    )
    dma = pltpu.SemaphoreType.DMA
    shapes = [
        ((3, 2, 32, 4096), F32),
        ((256, LANES), F32),
        ((256, LANES), F32),
        ((128 * BLOCK, LANES), F32),
        ((32 * PITCH, LANES), F32),
        ((32 * PITCH, LANES), F32),
        ((128 * BLOCK, LANES), F32),
        ((128, LANES), F32),
        ((128, LANES), F32),
        ((256, 256), F32),
        ((ROWS, 256, 2048), BF16),
        ((512, 768), BF16),
        ((64 * PITCH, LANES), F32),
        ((64 * PITCH, LANES), F32),
        ((4, 64 * PITCH, LANES), F32),
        ((256, 256), BF16),
    ] + [(value.shape, value.dtype) for value in values]
    return pl.pallas_call(
        kernel,
        out_shape=jax.ShapeDtypeStruct(current.shape, F32),
        in_specs=[smem, smem, vmem, vmem, vmem, anywhere] + [anywhere] * len(values),
        out_specs=vmem,
        scratch_shapes=[pltpu.VMEM(*shape) for shape in shapes]
        + [
            dma((len(values) + 1,)),
            dma((6,)),
            dma((ROWS,)),
            dma((2,)),
            dma((2,)),
            dma,
            pltpu.SemaphoreType.REGULAR,
        ],
        compiler_params=pltpu.CompilerParams(
            collective_id=0, has_side_effects=True, vmem_limit_bytes=58 * 1024 * 1024
        ),
    )(owner, resist, current, voxel, material, green, *values)


def solution(mesh):
    in_specs = (
        P(("row", "col"), None),
        P(("row", "col")),
        P(("row", "col"), None),
        P(("row", "col"), None),
        P(),
        P(None, None, ("row", "col"), None),
    )
    out_specs = P(("row", "col"), None)
    return jax.shard_map(shards, mesh=mesh, in_specs=in_specs, out_specs=out_specs, check_vma=False)
```

```python
import functools
import math

import jax
import jax.numpy as jnp
import ml_dtypes
import numpy as np
from jax import lax
from jax.experimental import pallas as pl
from jax.experimental.pallas import tpu as pltpu
from jax.sharding import PartitionSpec as P

F32 = jnp.float32
BF16 = jnp.bfloat16
LANES = 128


def halves(table):
    high = table.astype(ml_dtypes.bfloat16)
    low = (table - high.astype(np.float64)).astype(ml_dtypes.bfloat16)
    return high, low


def stacked(table, axis):
    high, low = halves(table)
    return np.concatenate([high, high, low], axis=axis)


def angles(left, right, length):
    return 2.0 * math.pi * (np.outer(left, right) % length) / length


@functools.lru_cache(maxsize=None)
def tables():
    out = {}
    j32, a16, n128, n64, a32 = (np.arange(n) for n in (32, 16, 128, 64, 32))
    theta = angles(j32, a16, 32)
    out["y_first"] = stacked(np.concatenate([np.cos(theta), -np.sin(theta)], axis=0), 1)
    theta = angles(j32, n128, 4096)
    out["y_turn"] = np.stack([np.cos(theta), -np.sin(theta)]).astype(np.float32)
    theta = angles(n128, n128, 128)
    cosine, sine = np.cos(theta), np.sin(theta)
    out["y_second"] = stacked(np.block([[cosine, -sine], [sine, cosine]]), 0)
    out["y_back"] = stacked(np.concatenate([cosine, sine], axis=0), 1)
    theta = np.tile(angles(n128, j32, 4096), (1, 4))
    sign = np.where(np.arange(128) < 64, -1.0, 1.0)
    out["y_unturn"] = np.stack([np.cos(theta), np.sin(theta) * sign]).astype(np.float32)
    theta = angles(j32, a16, 32)
    last = np.zeros((4, 2, 2, 32, 4, 2, 16))
    for x in range(4):
        for z in range(2):
            last[x, 0, z, :, x, z, :] = np.cos(theta)
            last[x, 1, z, :, x, z, :] = -np.sin(theta)
    out["y_last"] = stacked(last.reshape(512, 128), 0)
    first = []
    final = []
    for b in range(64):
        theta = angles(n64, 64 * a32 + b, 4096)
        first.append(stacked(np.concatenate([np.cos(theta), np.sin(theta)], axis=0), 1))
        final.append(stacked(np.concatenate([np.cos(theta.T), np.sin(theta.T)], axis=0), 1))
    out["x_first"] = np.concatenate(first, axis=0)
    out["x_final"] = np.concatenate(final, axis=0)
    theta = angles(n64, n64, 64)
    out["x_mid"] = stacked(np.concatenate([np.cos(theta), np.sin(theta)], axis=0), 1)
    return out


def split(value):
    high = value.astype(BF16)
    return high, (value - high.astype(F32)).astype(BF16)


MESH = pl.DeviceIdType.MESH
ROWS, COLS, EDGE = 8, 16, 4
PITCH, BLOCK = 72, 24
NAMES = (
    "y_first", "y_turn", "y_second", "x_first", "x_mid", "x_final", "y_back", "y_unturn", "y_last",
)


def dot(left, right, dims=(((1,), (0,)), ((), ()))):
    return lax.dot_general(left, right, dims, preferred_element_type=F32)


def triple(value):
    high, low = split(value)
    return jnp.concatenate([high, low, high], axis=0)


def combine(product, place, low):
    count = product.shape[0] // 2
    cosine = product[:count, LANES * place : LANES * place + LANES]
    sine = product[count:, LANES * place : LANES * place + LANES]
    lane = lax.broadcasted_iota(jnp.int32, (count, LANES), 1)
    sign = jnp.where(lane < LANES // 2, low, -low).astype(F32)
    return cosine + pltpu.roll(sine, LANES // 2, 1) * sign


def aligned(value, step):
    return pl.multiple_of(value * step, step)


def kernel(
    owner_ref, resist_ref, current_ref, voxel_ref, material_ref, green_hbm, *rest
):
    count = len(NAMES)
    tables_hbm, out_ref = rest[:count], rest[count]
    (
        green_ref, route_out, route_in, spread_ref, pencil_ref, field_out, field_in, picked_ref, returned_ref,
        slab_ref, top_ref, left_ref, half_ref, back_ref, coef_ref, volume_ref,
    ) = rest[count + 1 : count + 17]
    held = rest[count + 17 : 2 * count + 17]
    load_sems, send_sems, route_sems, pencil_sems, field_sems, return_sem = rest[2 * count + 17 :]
    first_y, turn_ref, second_y, first_x, mid_x, final_x, back_y, unturn_ref, last_y = held

    row, col = lax.axis_index("row"), lax.axis_index("col")
    me = row * COLS + col
    high_col, low_col = lax.div(col, EDGE), lax.rem(col, EDGE)

    barrier = pltpu.get_barrier_semaphore()
    far = (2, 1, 3, 0)
    all_cols = [lax.rem(high_col + y, EDGE) * EDGE + lax.rem(low_col + x, EDGE) for y in far for x in far]
    far_cols = all_cols[:-1]
    for r in (4, 3, 5, 2, 6, 1, 7, 0):
        to_row = lax.rem(row + r, ROWS)
        for to_col in all_cols if r else far_cols:
            pl.semaphore_signal(barrier, inc=1, device_id=(to_row, to_col), device_id_type=MESH)

    loads = [pltpu.make_async_copy(green_hbm, green_ref, load_sems.at[count])]
    loads += [pltpu.make_async_copy(tables_hbm[i], held[i], load_sems.at[i]) for i in range(count)]
    for load in loads:
        load.start()

    voxel = voxel_ref[...]
    live = voxel >= 0
    loaded = jnp.where(live, current_ref[...], 0.0)
    cells = voxel.astype(F32)
    values = jnp.zeros((ROWS * COLS, LANES), F32)
    places = jnp.full((ROWS * COLS, LANES), -1.0, F32)
    ids = lax.broadcasted_iota(jnp.int32, values.shape, 0)
    for block in range(current_ref.shape[0]):
        mine = ids == owner_ref[block]
        values = jnp.where(mine, loaded[block : block + 1], values)
        places = jnp.where(mine, cells[block : block + 1], places)
    route_out[pl.ds(0, ROWS * COLS, stride=2), :] = values
    route_out[pl.ds(1, ROWS * COLS, stride=2), :] = places
    pl.semaphore_wait(barrier, ROWS * COLS - 1)

    def remote(source, start, target, place, size, device, send_sem, recv_sem):
        return pltpu.make_async_remote_copy(
            source.at[pl.ds(start, size)],
            target.at[pl.ds(place, size)],
            send_sem,
            recv_sem,
            device_id=device,
            device_id_type=MESH,
        )

    def local(source, start, target, place, size, recv_sem):
        return pltpu.make_async_copy(source.at[pl.ds(start, size)], target.at[pl.ds(place, size)], recv_sem)

    def outward(k, middle):
        return middle + (1 - 2 * lax.rem(k, 2)) * lax.div(k + 1, 2)

    def in_row(to_col):
        return lax.div(to_col, EDGE) * PITCH + lax.rem(to_col, EDGE) * 16

    own_x = row * (EDGE * PITCH) + in_row(col)
    own_block = me * BLOCK

    def arrival(ref, rows, sem):
        part = ref.at[pl.ds(0, rows)]
        pltpu.make_async_copy(part, part, sem).wait()

    far_places = [in_row(to_col) for to_col in far_cols]
    own_place = in_row(col)
    next_cols = [lax.rem(col + k, COLS) for k in range(1, COLS)]

    def route(to_row, to_col, r):
        start = 2 * (to_row * COLS + to_col)
        remote(route_out, start, route_in, 2 * me, 2, (to_row, to_col), send_sems.at[0], route_sems.at[r]).start()

    for to_col in next_cols:
        route(row, to_col, 0)
    local(route_out, 2 * me, route_in, 2 * me, 2, route_sems.at[0]).start()
    for r in range(1, ROWS):
        route(lax.rem(row + r, ROWS), col, r)

    @pl.loop(0, ROWS - 1)
    def _(k):
        r = outward(k, ROWS // 2)
        to_row = lax.rem(row + r, ROWS)
        for to_col in far_cols:
            route(to_row, to_col, r)

    def to_all(send):
        @pl.loop(0, ROWS)
        def _(k):
            core = lax.rem(row + 1 + lax.div(k, 4), 2)
            to_row = 2 * lax.rem(lax.div(row, 2) + outward(lax.rem(k, 4), 2), 4) + core
            for to_col, place in zip(far_cols, far_places):
                send(to_row, to_col, place)

            @pl.when(to_row != row)
            def _():
                send(to_row, col, own_place)

    side = lax.broadcasted_iota(jnp.int32, (256, LANES), 0).astype(F32).astype(BF16)
    one, zero = jnp.ones((256, LANES), BF16), jnp.zeros((256, LANES), BF16)

    def asked(step):
        block = route_in[pl.ds(aligned(lax.rem(row - step + ROWS, ROWS), 2 * COLS), 2 * COLS), :]
        return block, block.astype(jnp.int32)

    for half in range(2):
        slab_ref[...] = jnp.zeros_like(slab_ref)

        @pl.loop(0, ROWS)
        def _(k):
            step = lax.rem(outward(lax.rem(k + ROWS - 1, ROWS), ROWS // 2), ROWS)
            if half == 0:
                arrival(route_in, 2 * COLS, route_sems.at[step])
            block, place = asked(step)
            top = jnp.where(place < 0, -1, (place >> 7) & 255).astype(F32).astype(BF16)
            spot = jnp.where((place >> 15) == half, place & 127, -1).astype(F32).astype(BF16)
            high, low = split(block)
            spots = []
            for s in range(COLS):
                if half == 0:
                    top_ref[step, :, LANES * s : LANES * s + LANES] = jnp.where(
                        side == top[2 * s + 1 : 2 * s + 2], one, zero
                    )
                hit = side[:LANES] == spot[2 * s + 1 : 2 * s + 2]
                spots.append(
                    jnp.concatenate(
                        [
                            jnp.where(hit, high[2 * s : 2 * s + 1], zero[:LANES]),
                            jnp.where(hit, low[2 * s : 2 * s + 1], zero[:LANES]),
                        ],
                        axis=0,
                    )
                )
            slab_ref[...] += dot(jnp.concatenate(spots, axis=1), top_ref[step], (((1,), (1,)), ((), ())))

        if half == 0:
            for load in loads[1:]:
                load.wait()
        slab = (slab_ref[:LANES, :] + slab_ref[LANES:, :]).T
        wide = jnp.concatenate([slab[16 * i : 16 * i + 16] for i in range(16)], axis=1)
        begun = dot(first_y[...], triple(wide))
        turn_re, turn_im = turn_ref[0], turn_ref[1]
        for i in range(16):
            re = begun[:32, LANES * i : LANES * i + LANES]
            im = begun[32:, LANES * i : LANES * i + LANES]
            both = jnp.concatenate([re * turn_re - im * turn_im, re * turn_im + im * turn_re], axis=1)
            high, low = split(both)
            left_ref[32 * i : 32 * i + 32, :] = jnp.concatenate([high, low, high], axis=1)
        spectra = dot(left_ref[...], second_y[...])
        for x in range(8):
            part = spectra[64 * x : 64 * x + 64]
            part = jnp.concatenate([part[:, :LANES], part[:, LANES:]], axis=0)
            spread_ref[pl.ds(8 * half + x, LANES, stride=BLOCK), :] = part.T

        def send(to_row, to_col, place):
            start = pl.multiple_of((to_row * COLS + to_col) * BLOCK + 8 * half, 8)
            remote(
                spread_ref, start, pencil_ref, pl.multiple_of(own_x + 8 * half, 8), 8, (to_row, to_col),
                send_sems.at[1 + half], pencil_sems.at[half],
            ).start()

        to_all(send)
        local(
            spread_ref, pl.multiple_of(own_block + 8 * half, 8), pencil_ref, pl.multiple_of(own_x + 8 * half, 8), 8,
            pencil_sems.at[half],
        ).start()

    loads[0].wait()

    @pl.loop(0, 32)
    def _(tile):
        cols = pl.ds(aligned(tile, LANES), LANES)
        re = [green_ref[o, 0, :, cols] for o in range(3)]
        im = [green_ref[o, 1, :, cols] for o in range(3)]
        arranged = [
            [re[1], re[1], re[1], re[1]],
            [re[0], -im[2], re[0], im[2]],
            [im[1], im[1], -im[1], -im[1]],
            [im[0], re[2], -im[0], re[2]],
        ]
        for g in range(4):
            turned = jnp.concatenate(arranged[g], axis=0).T
            coef_ref[g, pl.ds(2 * tile, 64, stride=PITCH), :] = turned[:64]
            coef_ref[g, pl.ds(2 * tile + 1, 64, stride=PITCH), :] = turned[64:]

    for half in range(2):
        arrival(pencil_ref, 1024, pencil_sems.at[half])
        for b in range(64):
            if (b % 16) // 8 == half:
                rows = pencil_ref[pl.ds(b, 32, stride=PITCH), :]
                product = dot(first_x[128 * b : 128 * b + 128, :], triple(rows))
                half_ref[pl.ds(b, 64, stride=PITCH), :] = combine(product, 0, 1.0)

    mid = mid_x[...]
    for start in range(0, 64, 8):
        ks = range(start, start + 8)
        product = dot(
            mid, jnp.concatenate([triple(half_ref[PITCH * k : PITCH * k + 64, :]) for k in ks], axis=1)
        )
        mixed = []
        for i, k in enumerate(ks):
            spectrum = combine(product, i, 1.0)
            aside = pltpu.roll(spectrum, LANES - 32, 1)
            near, far_part = [
                coef_ref[g, PITCH * k : PITCH * k + 64, :] * spectrum
                + coef_ref[g + 1, PITCH * k : PITCH * k + 64, :] * aside
                for g in (0, 2)
            ]
            total = near + pltpu.roll(far_part, LANES // 2, 1)
            mixed.append(triple(total))
        product = dot(mid, jnp.concatenate(mixed, axis=1))
        for i, k in enumerate(ks):
            back_ref[pl.ds(k, 64, stride=PITCH), :] = combine(product, i, -1.0)

    for half in range(2):
        for b in range(64):
            if (b % 16) // 8 == half:
                product = dot(final_x[64 * b : 64 * b + 64, :], triple(back_ref[PITCH * b : PITCH * b + 64, :]))
                field_out[pl.ds(b, 32, stride=PITCH), :] = combine(product, 0, -1.0)

        def send(to_row, to_col, place):
            start = pl.multiple_of(to_row * (EDGE * PITCH) + place + 8 * half, 8)
            remote(
                field_out, start, field_in, pl.multiple_of(own_block + 8 * half, 8), 8, (to_row, to_col),
                send_sems.at[3 + half], field_sems.at[half],
            ).start()

        to_all(send)
        local(
            field_out, pl.multiple_of(own_x + 8 * half, 8), field_in, pl.multiple_of(own_block + 8 * half, 8), 8,
            field_sems.at[half],
        ).start()

    cosine, sine = unturn_ref[0], unturn_ref[1]
    spots = lax.broadcasted_iota(jnp.int32, (LANES, LANES), 0)
    for half in range(2):
        arrival(field_in, 1024, field_sems.at[half])
        back = back_y[...]
        pieces = []
        for quad in range(2 * half, 2 * half + 2):
            product = dot(
                back,
                jnp.concatenate(
                    [triple(field_in[pl.ds(4 * quad + i, LANES, stride=BLOCK), :]) for i in range(4)], axis=1
                ),
            )
            turned = []
            for i in range(4):
                piece = combine(product, i, -1.0)
                turned.append(piece * cosine + pltpu.roll(piece, LANES // 2, 1) * sine)
            high, low = split(jnp.concatenate(turned, axis=1))
            pieces.append(dot(jnp.concatenate([high, low, high], axis=1), last_y[...]))
        volume_ref[...] = jnp.concatenate(split(jnp.concatenate(pieces, axis=1) * (1.0 / 16777216.0)), axis=0)

        @pl.loop(0, ROWS)
        def _(k):
            step = outward(k, ROWS // 2)
            base = lax.rem(row - step + ROWS, ROWS)
            block, place = asked(step)
            spot = jnp.where((place >> 15) == half, place & 127, -1)
            found = dot(volume_ref[...], top_ref[step])
            lines = []
            for s in range(COLS):
                line = found[:LANES, LANES * s : LANES * s + LANES] + found[LANES:, LANES * s : LANES * s + LANES]
                line = jnp.where(spots == spot[2 * s + 1 : 2 * s + 2], line, 0.0)
                lines.append(jnp.sum(line, axis=0, keepdims=True))
            lines = jnp.concatenate(lines, axis=0)
            rows = pl.ds(aligned(base, COLS), COLS)
            if half == 0:
                picked_ref[rows, :] = lines
            else:
                picked_ref[rows, :] += lines

                @pl.when(k == ROWS - 1)
                def _():
                    local(picked_ref, me, returned_ref, me, 1, return_sem).start()

                for to_col in far_cols:
                    remote(
                        picked_ref, base * COLS + to_col, returned_ref, me, 1, (base, to_col), send_sems.at[5], return_sem
                    ).start()

                @pl.when(k < ROWS - 1)
                def _():
                    remote(
                        picked_ref, base * COLS + col, returned_ref, me, 1, (base, col), send_sems.at[5], return_sem
                    ).start()

    rates = jnp.zeros(current_ref.shape, F32)
    for kind in range(8):
        rates = jnp.where(material_ref[...] == kind, resist_ref[kind], rates)
    own = rates * current_ref[...]
    pltpu.make_async_copy(returned_ref, returned_ref, return_sem).wait()
    coupled = jnp.concatenate(
        [returned_ref[pl.ds(owner_ref[b], 1), :] for b in range(current_ref.shape[0])], axis=0
    )
    out_ref[...] = jnp.where(live, own + coupled, 0.0)
    for i, (ref, size) in enumerate(
        ((route_out, 2), (spread_ref, 8), (spread_ref, 8), (field_out, 8), (field_out, 8), (picked_ref, 1))
    ):
        arrival(ref, (ROWS * COLS - 1) * size, send_sems.at[i])


def shards(current, owner, voxel, material, resist, green):
    values = [jnp.asarray(tables()[name]) for name in NAMES]
    vmem, smem, anywhere = (
        pl.BlockSpec(memory_space=space) for space in (pltpu.VMEM, pltpu.SMEM, pl.ANY)
    )
    dma = pltpu.SemaphoreType.DMA
    shapes = [
        ((3, 2, 32, 4096), F32),
        ((256, LANES), F32),
        ((256, LANES), F32),
        ((128 * BLOCK, LANES), F32),
        ((32 * PITCH, LANES), F32),
        ((32 * PITCH, LANES), F32),
        ((128 * BLOCK, LANES), F32),
        ((128, LANES), F32),
        ((128, LANES), F32),
        ((256, 256), F32),
        ((ROWS, 256, 2048), BF16),
        ((512, 768), BF16),
        ((64 * PITCH, LANES), F32),
        ((64 * PITCH, LANES), F32),
        ((4, 64 * PITCH, LANES), F32),
        ((256, 256), BF16),
    ] + [(value.shape, value.dtype) for value in values]
    return pl.pallas_call(
        kernel,
        out_shape=jax.ShapeDtypeStruct(current.shape, F32),
        in_specs=[smem, smem, vmem, vmem, vmem, anywhere] + [anywhere] * len(values),
        out_specs=vmem,
        scratch_shapes=[pltpu.VMEM(*shape) for shape in shapes]
        + [
            dma((len(values) + 1,)),
            dma((6,)),
            dma((ROWS,)),
            dma((2,)),
            dma((2,)),
            dma,
        ],
        compiler_params=pltpu.CompilerParams(
            collective_id=0, has_side_effects=True, vmem_limit_bytes=58 * 1024 * 1024
        ),
    )(owner, resist, current, voxel, material, green, *values)


def solution(mesh):
    in_specs = (
        P(("row", "col"), None),
        P(("row", "col")),
        P(("row", "col"), None),
        P(("row", "col"), None),
        P(),
        P(None, None, ("row", "col"), None),
    )
    out_specs = P(("row", "col"), None)
    return jax.shard_map(shards, mesh=mesh, in_specs=in_specs, out_specs=out_specs, check_vma=False)
```

```python
import functools
import math

import jax
import jax.numpy as jnp
import ml_dtypes
import numpy as np
from jax import lax
from jax.experimental import pallas as pl
from jax.experimental.pallas import tpu as pltpu
from jax.sharding import PartitionSpec as P

F32 = jnp.float32
BF16 = jnp.bfloat16
LANES = 128


def halves(table):
    high = table.astype(ml_dtypes.bfloat16)
    low = (table - high.astype(np.float64)).astype(ml_dtypes.bfloat16)
    return high, low


def stacked(table, axis):
    high, low = halves(table)
    return np.concatenate([high, high, low], axis=axis)


def angles(left, right, length):
    return 2.0 * math.pi * (np.outer(left, right) % length) / length


@functools.lru_cache(maxsize=None)
def tables():
    out = {}
    j32, a16, n128, n64, a32 = (np.arange(n) for n in (32, 16, 128, 64, 32))
    theta = angles(j32, a16, 32)
    out["y_first"] = stacked(np.concatenate([np.cos(theta), -np.sin(theta)], axis=0), 1)
    theta = angles(j32, n128, 4096)
    out["y_turn"] = np.stack([np.cos(theta), -np.sin(theta)]).astype(np.float32)
    theta = angles(n128, n128, 128)
    cosine, sine = np.cos(theta), np.sin(theta)
    out["y_second"] = stacked(np.block([[cosine, -sine], [sine, cosine]]), 0)
    out["y_back"] = stacked(np.concatenate([cosine, sine], axis=0), 1)
    theta = np.tile(angles(n128, j32, 4096), (1, 4))
    sign = np.where(np.arange(128) < 64, -1.0, 1.0)
    out["y_unturn"] = np.stack([np.cos(theta), np.sin(theta) * sign]).astype(np.float32)
    theta = angles(j32, a16, 32)
    last = np.zeros((4, 2, 2, 32, 4, 2, 16))
    for x in range(4):
        for z in range(2):
            last[x, 0, z, :, x, z, :] = np.cos(theta)
            last[x, 1, z, :, x, z, :] = -np.sin(theta)
    out["y_last"] = stacked(last.reshape(512, 128), 0)
    first = []
    final = []
    for b in range(64):
        theta = angles(n64, 64 * a32 + b, 4096)
        first.append(stacked(np.concatenate([np.cos(theta), np.sin(theta)], axis=0), 1))
        final.append(stacked(np.concatenate([np.cos(theta.T), np.sin(theta.T)], axis=0), 1))
    out["x_first"] = np.concatenate(first, axis=0)
    out["x_final"] = np.concatenate(final, axis=0)
    theta = angles(n64, n64, 64)
    out["x_mid"] = stacked(np.concatenate([np.cos(theta), np.sin(theta)], axis=0), 1)
    return out


def split(value):
    high = value.astype(BF16)
    return high, (value - high.astype(F32)).astype(BF16)


MESH = pl.DeviceIdType.MESH
ROWS, COLS, EDGE = 8, 16, 4
PITCH, BLOCK = 72, 24
NAMES = (
    "y_first", "y_turn", "y_second", "x_first", "x_mid", "x_final", "y_back", "y_unturn", "y_last",
)


def dot(left, right, dims=(((1,), (0,)), ((), ()))):
    return lax.dot_general(left, right, dims, preferred_element_type=F32)


def triple(value):
    high, low = split(value)
    return jnp.concatenate([high, low, high], axis=0)


def combine(product, place, low):
    count = product.shape[0] // 2
    cosine = product[:count, LANES * place : LANES * place + LANES]
    sine = product[count:, LANES * place : LANES * place + LANES]
    lane = lax.broadcasted_iota(jnp.int32, (count, LANES), 1)
    sign = jnp.where(lane < LANES // 2, low, -low).astype(F32)
    return cosine + pltpu.roll(sine, LANES // 2, 1) * sign


def aligned(value, step):
    return pl.multiple_of(value * step, step)


def kernel(
    owner_ref, resist_ref, current_ref, voxel_ref, material_ref, green_hbm, *rest
):
    count = len(NAMES)
    tables_hbm, out_ref = rest[:count], rest[count]
    (
        green_ref, route_out, route_in, spread_ref, pencil_ref, field_out, field_in, picked_ref, returned_ref,
        slab_ref, top_ref, left_ref, half_ref, back_ref, coef_ref, volume_ref,
    ) = rest[count + 1 : count + 17]
    held = rest[count + 17 : 2 * count + 17]
    load_sems, send_sems, route_sems, pencil_sems, field_sems, return_sem = rest[2 * count + 17 :]
    first_y, turn_ref, second_y, first_x, mid_x, final_x, back_y, unturn_ref, last_y = held

    row, col = lax.axis_index("row"), lax.axis_index("col")
    me = row * COLS + col
    high_col, low_col = lax.div(col, EDGE), lax.rem(col, EDGE)

    barrier = pltpu.get_barrier_semaphore()
    far = (2, 1, 3, 0)
    all_cols = [lax.rem(high_col + y, EDGE) * EDGE + lax.rem(low_col + x, EDGE) for y in far for x in far]
    far_cols = all_cols[:-1]
    for r in (4, 3, 5, 2, 6, 1, 7, 0):
        to_row = lax.rem(row + r, ROWS)
        for to_col in all_cols if r else far_cols:
            pl.semaphore_signal(barrier, inc=1, device_id=(to_row, to_col), device_id_type=MESH)

    loads = [pltpu.make_async_copy(green_hbm, green_ref, load_sems.at[count])]
    loads += [pltpu.make_async_copy(tables_hbm[i], held[i], load_sems.at[i]) for i in range(count)]
    for load in loads:
        load.start()

    voxel = voxel_ref[...]
    live = voxel >= 0
    loaded = jnp.where(live, current_ref[...], 0.0)
    cells = voxel.astype(F32)
    values = jnp.zeros((ROWS * COLS, LANES), F32)
    places = jnp.full((ROWS * COLS, LANES), -1.0, F32)
    ids = lax.broadcasted_iota(jnp.int32, values.shape, 0)
    for block in range(current_ref.shape[0]):
        mine = ids == owner_ref[block]
        values = jnp.where(mine, loaded[block : block + 1], values)
        places = jnp.where(mine, cells[block : block + 1], places)
    route_out[pl.ds(0, ROWS * COLS, stride=2), :] = values
    route_out[pl.ds(1, ROWS * COLS, stride=2), :] = places
    pl.semaphore_wait(barrier, ROWS * COLS - 1)

    def remote(source, start, target, place, size, device, send_sem, recv_sem):
        return pltpu.make_async_remote_copy(
            source.at[pl.ds(start, size)],
            target.at[pl.ds(place, size)],
            send_sem,
            recv_sem,
            device_id=device,
            device_id_type=MESH,
        )

    def local(source, start, target, place, size, recv_sem):
        return pltpu.make_async_copy(source.at[pl.ds(start, size)], target.at[pl.ds(place, size)], recv_sem)

    def outward(k, middle):
        return middle + (1 - 2 * lax.rem(k, 2)) * lax.div(k + 1, 2)

    def in_row(to_col):
        return lax.div(to_col, EDGE) * PITCH + lax.rem(to_col, EDGE) * 16

    own_x = row * (EDGE * PITCH) + in_row(col)
    own_block = me * BLOCK

    def arrival(ref, rows, sem):
        part = ref.at[pl.ds(0, rows)]
        pltpu.make_async_copy(part, part, sem).wait()

    far_places = [in_row(to_col) for to_col in far_cols]
    own_place = in_row(col)
    next_cols = [lax.rem(col + k, COLS) for k in range(1, COLS)]

    def route(to_row, to_col, r):
        start = 2 * (to_row * COLS + to_col)
        remote(route_out, start, route_in, 2 * me, 2, (to_row, to_col), send_sems.at[0], route_sems.at[r]).start()

    for to_col in next_cols:
        route(row, to_col, 0)
    local(route_out, 2 * me, route_in, 2 * me, 2, route_sems.at[0]).start()
    for r in range(1, ROWS):
        route(lax.rem(row + r, ROWS), col, r)

    @pl.loop(0, ROWS - 1)
    def _(k):
        r = outward(k, ROWS // 2)
        to_row = lax.rem(row + r, ROWS)
        for to_col in far_cols:
            route(to_row, to_col, r)

    def to_all(send):
        @pl.loop(0, ROWS)
        def _(k):
            core = lax.rem(row + 1 + lax.div(k, 4), 2)
            to_row = 2 * lax.rem(lax.div(row, 2) + outward(lax.rem(k, 4), 2), 4) + core
            for to_col, place in zip(far_cols, far_places):
                send(to_row, to_col, place)

            @pl.when(to_row != row)
            def _():
                send(to_row, col, own_place)

    side = lax.broadcasted_iota(jnp.int32, (256, LANES), 0).astype(F32).astype(BF16)
    one, zero = jnp.ones((256, LANES), BF16), jnp.zeros((256, LANES), BF16)

    def asked(step):
        block = route_in[pl.ds(aligned(lax.rem(row - step + ROWS, ROWS), 2 * COLS), 2 * COLS), :]
        return block, block.astype(jnp.int32)

    for half in range(2):
        slab_ref[...] = jnp.zeros_like(slab_ref)

        @pl.loop(0, ROWS)
        def _(k):
            step = lax.rem(outward(lax.rem(k + ROWS - 1, ROWS), ROWS // 2), ROWS)
            if half == 0:
                arrival(route_in, 2 * COLS, route_sems.at[step])
            block, place = asked(step)
            top = jnp.where(place < 0, -1, (place >> 7) & 255).astype(F32).astype(BF16)
            spot = jnp.where((place >> 15) == half, place & 127, -1).astype(F32).astype(BF16)
            high, low = split(block)
            spots = []
            for s in range(COLS):
                if half == 0:
                    top_ref[step, :, LANES * s : LANES * s + LANES] = jnp.where(
                        side == top[2 * s + 1 : 2 * s + 2], one, zero
                    )
                hit = side[:LANES] == spot[2 * s + 1 : 2 * s + 2]
                spots.append(
                    jnp.concatenate(
                        [
                            jnp.where(hit, high[2 * s : 2 * s + 1], zero[:LANES]),
                            jnp.where(hit, low[2 * s : 2 * s + 1], zero[:LANES]),
                        ],
                        axis=0,
                    )
                )
            slab_ref[...] += dot(jnp.concatenate(spots, axis=1), top_ref[step], (((1,), (1,)), ((), ())))

        if half == 0:
            for load in loads[1:]:
                load.wait()
        slab = (slab_ref[:LANES, :] + slab_ref[LANES:, :]).T
        wide = jnp.concatenate([slab[16 * i : 16 * i + 16] for i in range(16)], axis=1)
        begun = dot(first_y[...], triple(wide))
        turn_re, turn_im = turn_ref[0], turn_ref[1]
        for i in range(16):
            re = begun[:32, LANES * i : LANES * i + LANES]
            im = begun[32:, LANES * i : LANES * i + LANES]
            both = jnp.concatenate([re * turn_re - im * turn_im, re * turn_im + im * turn_re], axis=1)
            high, low = split(both)
            left_ref[32 * i : 32 * i + 32, :] = jnp.concatenate([high, low, high], axis=1)
        spectra = dot(left_ref[...], second_y[...])
        for x in range(8):
            part = spectra[64 * x : 64 * x + 64]
            part = jnp.concatenate([part[:, :LANES], part[:, LANES:]], axis=0)
            spread_ref[pl.ds(8 * half + x, LANES, stride=BLOCK), :] = part.T

        def send(to_row, to_col, place):
            start = pl.multiple_of((to_row * COLS + to_col) * BLOCK + 8 * half, 8)
            remote(
                spread_ref, start, pencil_ref, pl.multiple_of(own_x + 8 * half, 8), 8, (to_row, to_col),
                send_sems.at[1 + half], pencil_sems.at[half],
            ).start()

        to_all(send)
        local(
            spread_ref, pl.multiple_of(own_block + 8 * half, 8), pencil_ref, pl.multiple_of(own_x + 8 * half, 8), 8,
            pencil_sems.at[half],
        ).start()

    loads[0].wait()

    @pl.loop(0, 32)
    def _(tile):
        cols = pl.ds(aligned(tile, LANES), LANES)
        re = [green_ref[o, 0, :, cols] for o in range(3)]
        im = [green_ref[o, 1, :, cols] for o in range(3)]
        arranged = [
            [re[1], re[1], re[1], re[1]],
            [re[0], -im[2], re[0], im[2]],
            [im[1], im[1], -im[1], -im[1]],
            [im[0], re[2], -im[0], re[2]],
        ]
        for g in range(4):
            turned = jnp.concatenate(arranged[g], axis=0).T
            coef_ref[g, pl.ds(2 * tile, 64, stride=PITCH), :] = turned[:64]
            coef_ref[g, pl.ds(2 * tile + 1, 64, stride=PITCH), :] = turned[64:]

    for half in range(2):
        arrival(pencil_ref, 1024, pencil_sems.at[half])
        for b in range(64):
            if (b % 16) // 8 == half:
                rows = pencil_ref[pl.ds(b, 32, stride=PITCH), :]
                product = dot(first_x[128 * b : 128 * b + 128, :], triple(rows))
                half_ref[pl.ds(b, 64, stride=PITCH), :] = combine(product, 0, 1.0)

    mid = mid_x[...]
    for start in range(0, 64, 8):
        ks = range(start, start + 8)
        product = dot(
            mid, jnp.concatenate([triple(half_ref[PITCH * k : PITCH * k + 64, :]) for k in ks], axis=1)
        )
        mixed = []
        for i, k in enumerate(ks):
            spectrum = combine(product, i, 1.0)
            aside = pltpu.roll(spectrum, LANES - 32, 1)
            near, far_part = [
                coef_ref[g, PITCH * k : PITCH * k + 64, :] * spectrum
                + coef_ref[g + 1, PITCH * k : PITCH * k + 64, :] * aside
                for g in (0, 2)
            ]
            total = near + pltpu.roll(far_part, LANES // 2, 1)
            mixed.append(triple(total))
        product = dot(mid, jnp.concatenate(mixed, axis=1))
        for i, k in enumerate(ks):
            back_ref[pl.ds(k, 64, stride=PITCH), :] = combine(product, i, -1.0)

    for half in range(2):
        for b in range(64):
            if (b % 16) // 8 == half:
                product = dot(final_x[64 * b : 64 * b + 64, :], triple(back_ref[PITCH * b : PITCH * b + 64, :]))
                field_out[pl.ds(b, 32, stride=PITCH), :] = combine(product, 0, -1.0)

        def send(to_row, to_col, place):
            start = pl.multiple_of(to_row * (EDGE * PITCH) + place + 8 * half, 8)
            remote(
                field_out, start, field_in, pl.multiple_of(own_block + 8 * half, 8), 8, (to_row, to_col),
                send_sems.at[3 + half], field_sems.at[half],
            ).start()

        to_all(send)
        local(
            field_out, pl.multiple_of(own_x + 8 * half, 8), field_in, pl.multiple_of(own_block + 8 * half, 8), 8,
            field_sems.at[half],
        ).start()

    cosine, sine = unturn_ref[0], unturn_ref[1]
    spots = lax.broadcasted_iota(jnp.int32, (LANES, LANES), 0)
    for half in range(2):
        arrival(field_in, 1024, field_sems.at[half])
        back = back_y[...]
        pieces = []
        for quad in range(2 * half, 2 * half + 2):
            product = dot(
                back,
                jnp.concatenate(
                    [triple(field_in[pl.ds(4 * quad + i, LANES, stride=BLOCK), :]) for i in range(4)], axis=1
                ),
            )
            turned = []
            for i in range(4):
                piece = combine(product, i, -1.0)
                turned.append(piece * cosine + pltpu.roll(piece, LANES // 2, 1) * sine)
            high, low = split(jnp.concatenate(turned, axis=1))
            pieces.append(dot(jnp.concatenate([high, low, high], axis=1), last_y[...]))
        volume_ref[...] = jnp.concatenate(split(jnp.concatenate(pieces, axis=1) * (1.0 / 16777216.0)), axis=0)

        @pl.loop(0, ROWS)
        def _(k):
            step = outward(k, ROWS // 2)
            base = lax.rem(row - step + ROWS, ROWS)
            block, place = asked(step)
            spot = jnp.where((place >> 15) == half, place & 127, -1)
            found = dot(volume_ref[...], top_ref[step])
            lines = []
            for s in range(COLS):
                line = found[:LANES, LANES * s : LANES * s + LANES] + found[LANES:, LANES * s : LANES * s + LANES]
                line = jnp.where(spots == spot[2 * s + 1 : 2 * s + 2], line, 0.0)
                lines.append(jnp.sum(line, axis=0, keepdims=True))
            lines = jnp.concatenate(lines, axis=0)
            rows = pl.ds(aligned(base, COLS), COLS)
            if half == 0:
                picked_ref[rows, :] = lines
            else:
                picked_ref[rows, :] += lines

                @pl.when(k == ROWS - 1)
                def _():
                    local(picked_ref, me, returned_ref, me, 1, return_sem).start()

                for to_col in far_cols:
                    remote(
                        picked_ref, base * COLS + to_col, returned_ref, me, 1, (base, to_col), send_sems.at[5], return_sem
                    ).start()

                @pl.when(k < ROWS - 1)
                def _():
                    remote(
                        picked_ref, base * COLS + col, returned_ref, me, 1, (base, col), send_sems.at[5], return_sem
                    ).start()

    rates = jnp.zeros(current_ref.shape, F32)
    for kind in range(8):
        rates = jnp.where(material_ref[...] == kind, resist_ref[kind], rates)
    own = rates * current_ref[...]
    pltpu.make_async_copy(returned_ref, returned_ref, return_sem).wait()
    coupled = jnp.concatenate(
        [returned_ref[pl.ds(owner_ref[b], 1), :] for b in range(current_ref.shape[0])], axis=0
    )
    out_ref[...] = jnp.where(live, own + coupled, 0.0)
    for i, (ref, size) in enumerate(
        ((route_out, 2), (spread_ref, 8), (spread_ref, 8), (field_out, 8), (field_out, 8), (picked_ref, 1))
    ):
        arrival(ref, (ROWS * COLS - 1) * size, send_sems.at[i])


def shards(current, owner, voxel, material, resist, green):
    values = [jnp.asarray(tables()[name]) for name in NAMES]
    vmem, smem, anywhere = (
        pl.BlockSpec(memory_space=space) for space in (pltpu.VMEM, pltpu.SMEM, pl.ANY)
    )
    dma = pltpu.SemaphoreType.DMA
    shapes = [
        ((3, 2, 32, 4096), F32),
        ((256, LANES), F32),
        ((256, LANES), F32),
        ((128 * BLOCK, LANES), F32),
        ((32 * PITCH, LANES), F32),
        ((32 * PITCH, LANES), F32),
        ((128 * BLOCK, LANES), F32),
        ((128, LANES), F32),
        ((128, LANES), F32),
        ((256, 256), F32),
        ((ROWS, 256, 2048), BF16),
        ((512, 768), BF16),
        ((64 * PITCH, LANES), F32),
        ((64 * PITCH, LANES), F32),
        ((4, 65 * PITCH, LANES), F32),
        ((256, 256), BF16),
    ] + [(value.shape, value.dtype) for value in values]
    return pl.pallas_call(
        kernel,
        out_shape=jax.ShapeDtypeStruct(current.shape, F32),
        in_specs=[smem, smem, vmem, vmem, vmem, anywhere] + [anywhere] * len(values),
        out_specs=vmem,
        scratch_shapes=[pltpu.VMEM(*shape) for shape in shapes]
        + [
            dma((len(values) + 1,)),
            dma((6,)),
            dma((ROWS,)),
            dma((2,)),
            dma((2,)),
            dma,
        ],
        compiler_params=pltpu.CompilerParams(
            collective_id=0, has_side_effects=True, vmem_limit_bytes=58 * 1024 * 1024
        ),
    )(owner, resist, current, voxel, material, green, *values)


def solution(mesh):
    in_specs = (
        P(("row", "col"), None),
        P(("row", "col")),
        P(("row", "col"), None),
        P(("row", "col"), None),
        P(),
        P(None, None, ("row", "col"), None),
    )
    out_specs = P(("row", "col"), None)
    return jax.shard_map(shards, mesh=mesh, in_specs=in_specs, out_specs=out_specs, check_vma=False)
```
